256 devices in a mesh: row: 64 (over z_lo, x, y), col: 4 (over z_hi, core).
Axes of the slice: x: 4, y: 4, z: 8 (z_hi: 2, z_lo: 4; z = z_hi * 4 + z_lo), core: 2. Of those that a mesh axis runs over, the one named last changes fastest.
Arguments:
- features: float32 [65536, 256], P('row', 'col'), may hold values from -6 to 6
- weight: float32 [256, 256], replicated, may hold values from -0.375 to 0.375
- cotangent: float32 [65536, 256], P('row', 'col'), may hold values from -6 to 6
- degrees: int32 [65536], P('row'), may hold values from 1 to 16432, as said below
- tiles: int32 [8192, 128, 128], P('row'), may hold values from 0 to 1
- block_rows: int32 [8192], P('row'), may hold values from 0 to 7
- block_source: int32 [8192], P('row'), may hold values from 0 to 63
- block_slot: int32 [8192], P('row'), may hold values from 0 to 1
- block_count: int32 [64], P('row'), may hold values from 32 to 128, as said below
- pair_blocks: int32 [64, 64, 2], replicated, may hold values from 0 to 7, as said below
Outputs:
- output: float32 [65536, 256], P('row', 'col')
- h_grad: float32 [65536, 256], P('row', 'col')
- weight_grad: float32 [256, 256], P('col')
The draws below stay inside these ranges and needn't reach their ends.
Inputs may be any that keep to these rules, and one draw needn't show every extreme that they name: Within one row index the 128 triples (block_rows, block_source, block_slot) are distinct. `block_count`: each row index has 32 to 128 live slots; some row index has exactly 128. `pair_blocks`: for every destination and source the 2 entries are distinct. `degrees`: each node's degree exceeds its number of nonzeros in its row of A.
All inputs are finite; a program needn't handle non-finite values.
Results may differ from the reference program's by a relative error of at most 0.00015.
Values sent between devices are 32-bit elements; how exact they have to be, the bound alone decides.
No kernel may reach another device: no remote copies, remote signals or barrier semaphores. Data moves between devices by JAX's collectives and lax.ppermute only.
A program may use at most 128 MiB of HBM per device.

```python
import jax
import jax.numpy as jnp
from jax import lax

F = 256
BS = 128
RB = 8
P_SIZE = 2
BLK = 128
NODES = 65536
N_ROW = 64


def block_table(key):
    keys = jax.random.split(key, N_ROW)

    def one_device(device_key):
        return jax.random.permutation(device_key, RB * N_ROW * P_SIZE)[:BLK]
    return jax.vmap(one_device)(keys).reshape(-1).astype(jnp.int32)


def live_counts(key):
    key = jax.random.fold_in(key, 5)
    first_key, second_key = jax.random.split(key)
    counts = jax.random.randint(first_key, (N_ROW,), BLK // 4, BLK + 1)
    fullest = jax.random.randint(second_key, (), 0, N_ROW)
    return jnp.where(jnp.arange(N_ROW) == fullest, BLK, counts).astype(jnp.int32)


def tile_bits(key):
    key = jax.random.fold_in(key, 13)
    values = jax.random.randint(key, (N_ROW * BLK, BS, BS), 0, 64)
    return (values == 0).astype(jnp.int32)


def draw_block_rows(key, part):
    codes = block_table(key)
    return codes // (N_ROW * P_SIZE)


def draw_block_source(key, part):
    codes = block_table(key)
    return codes // P_SIZE % N_ROW


def draw_block_slot(key, part):
    codes = block_table(key)
    return codes % P_SIZE


def draw_block_count(key, part):
    return live_counts(key)


def draw_tiles(key, part):
    return tile_bits(key)


def draw_degrees(key, part):
    codes = block_table(key)
    counts = live_counts(key)
    bits = tile_bits(key)
    key = jax.random.fold_in(key, 17)
    extra_key, top_key = jax.random.split(key)
    rows_local = codes // (N_ROW * P_SIZE)
    slot_ids = jnp.arange(N_ROW * BLK, dtype=jnp.int32)
    owner = slot_ids // BLK
    live = (slot_ids % BLK < counts[owner]).astype(jnp.int32)
    row_sums = jnp.sum(bits, axis=2) * live[:, None]
    target = owner * RB + rows_local
    block_sums = jax.ops.segment_sum(row_sums, target, num_segments=NODES // BS)
    extra = jax.random.randint(extra_key, (NODES,), 1, 49)
    drawn = block_sums.reshape(-1) + extra
    top_node = jax.random.randint(top_key, (), 0, NODES)
    top_value = min(BLK, N_ROW * P_SIZE) * BS + 48
    return jnp.where(jnp.arange(NODES) == top_node, top_value, drawn).astype(jnp.int32)


def draw_pair_blocks(key, part):
    key = jax.random.fold_in(key, 7)
    keys = jax.random.split(key, N_ROW * N_ROW)

    def one_pair(pair_key):
        return jax.random.permutation(pair_key, RB)[:P_SIZE]
    return jax.vmap(one_pair)(keys).reshape(N_ROW, N_ROW, P_SIZE).astype(jnp.int32)


def block_levels(key, dims, cuts, low, largest):
    def one(dim, parts):
        draws = jax.random.uniform(jax.random.fold_in(jax.random.fold_in(key, 6), dim), (parts,), jnp.float32, low / len(cuts), largest / len(cuts))
        return jnp.repeat(jnp.exp(draws), dims[dim] // parts).reshape((-1,) + (1,) * (len(dims) - dim - 1))

    factor_of = one(*cuts[0])
    for cut in cuts[1:]:
        factor_of = factor_of * one(*cut)
    return factor_of


def centred(stream_key, shape, width, reach, pieces=(), held_as=jnp.bfloat16):
    entries = jax.random.normal(stream_key, shape, jnp.float32) * width
    if len(pieces) > 0:
        entries = block_levels(stream_key, shape, pieces, -0.22, 0.18) * entries
    return jnp.clip(entries, min=-reach, max=reach).astype(held_as)


def setup_inputs(seed: int = 0) -> dict:
    key_list = jax.random.split(jax.random.key(seed), 11)
    features = centred(key_list[0], (NODES, F), 1.0, 6.0, ((0, 64), (1, 4)), jnp.float32)
    weight = centred(key_list[1], (F, F), F ** -0.5, 0.375, (), jnp.float32)
    cotangent = centred(key_list[2], (NODES, F), 1.0, 6.0, ((0, 64), (1, 4)), jnp.float32)
    degrees = draw_degrees(jax.random.fold_in(key_list[10], 71), 0)
    tiles = draw_tiles(jax.random.fold_in(key_list[10], 71), 0)
    block_rows = draw_block_rows(jax.random.fold_in(key_list[10], 71), 0)
    block_source = draw_block_source(jax.random.fold_in(key_list[10], 71), 0)
    block_slot = draw_block_slot(jax.random.fold_in(key_list[10], 71), 0)
    block_count = draw_block_count(jax.random.fold_in(key_list[10], 71), 0)
    pair_blocks = draw_pair_blocks(jax.random.fold_in(key_list[10], 71), 0)
    return {"features": features, "weight": weight, "cotangent": cotangent, "degrees": degrees, "tiles": tiles, "block_rows": block_rows, "block_source": block_source, "block_slot": block_slot, "block_count": block_count, "pair_blocks": pair_blocks}


def reference(features, weight, cotangent, degrees, tiles, block_rows, block_source, block_slot, block_count, pair_blocks):
    highest = lax.Precision.HIGHEST
    degree_f = degrees.astype(jnp.float32)
    root_deg = lax.rsqrt(degree_f)
    inverse = 1.0 / degree_f
    devices = jnp.arange(N_ROW, dtype=jnp.int32)
    tile_set = tiles.reshape(N_ROW, BLK, BS, BS)
    row_index = block_rows.reshape(N_ROW, BLK)
    source = block_source.reshape(N_ROW, BLK)
    slot_index = block_slot.reshape(N_ROW, BLK)
    local_block = pair_blocks[devices[:, None], source, slot_index]
    column = source * RB + local_block
    live_mask = (jnp.arange(BLK, dtype=jnp.int32)[None, :] < block_count[:, None]).astype(jnp.float32)
    scaled = (features * root_deg[:, None]).reshape(NODES // BS, BS, F)

    def forward(inputs):
        tile_one, rows_one, column_one, mask_one = inputs
        adjacency = tile_one.astype(jnp.float32) * mask_one[:, None, None]
        picked = scaled[column_one]
        contrib = jnp.einsum('bij,bjw->biw', adjacency, picked, precision=highest)
        return jax.ops.segment_sum(contrib, rows_one, num_segments=RB)
    summed = lax.map(forward, (tile_set, row_index, column, live_mask)).reshape(NODES, F)
    aggregated = root_deg[:, None] * summed + features * inverse[:, None]
    preact = jnp.dot(aggregated, weight, precision=highest)
    output = jax.nn.silu(preact)
    sigmoid_z = jax.nn.sigmoid(preact)
    delta_z = cotangent * sigmoid_z * (1.0 + preact * (1.0 - sigmoid_z))
    weight_grad = jnp.dot(aggregated.T, delta_z, precision=highest) * NODES ** (-0.5)
    back_in = jnp.dot(delta_z, weight.T, precision=highest)
    back_scaled = (back_in * root_deg[:, None]).reshape(NODES // BS, BS, F)

    def backward(totals, inputs):
        device_one, tile_one, rows_one, column_one, mask_one = inputs
        adjacency = tile_one.astype(jnp.float32) * mask_one[:, None, None]
        picked = back_scaled[device_one * RB + rows_one]
        contrib = jnp.einsum('bji,bjw->biw', adjacency, picked, precision=highest)
        return (totals.at[column_one].add(contrib), None)
    totals = jnp.zeros((NODES // BS, BS, F), jnp.float32)
    totals, unused = lax.scan(backward, totals, (devices, tile_set, row_index, column, live_mask))
    h_grad = root_deg[:, None] * totals.reshape(NODES, F) + back_in * inverse[:, None]
    return (output, h_grad, weight_grad)
```

```python
import functools

import jax
import jax.numpy as jnp
from jax import lax
from jax.experimental import pallas as pl
from jax.experimental.pallas import tpu as pltpu
from jax.sharding import PartitionSpec as P

SIDE = 4
GROUP = 8
F32 = jnp.float32
BF16 = jnp.bfloat16
NT = (((1,), (1,)), ((), ()))
NN = (((1,), (0,)), ((), ()))
TN = (((0,), (0,)), ((), ()))


def row_id(z, x, y):
    return z * SIDE * SIDE + x * SIDE + y


def row_perm(move):
    box = range(SIDE)
    return [(row_id(z, x, y), row_id(*move(z, x, y))) for z in box for x in box for y in box]


def shift_x(value, d):
    return lax.ppermute(value, "row", row_perm(lambda z, x, y: (z, (x + d) % SIDE, y)))


def shift_y(value, d):
    return lax.ppermute(value, "row", row_perm(lambda z, x, y: (z, x, (y + d) % SIDE)))


def swap_z(value, k):
    return lax.ppermute(value, "row", row_perm(lambda z, x, y: (z ^ k, x, y)))


def swap_col(value, k):
    return lax.ppermute(value, "col", [(c, c ^ k) for c in range(4)])


def halves(value):
    high = value.astype(BF16)
    return high, (value - high.astype(F32)).astype(BF16)


def dot(a, b, dims):
    return lax.dot_general(a, b, dims, preferred_element_type=F32)


def dot3(a, b, dims):
    a_high, a_low = a
    b_high, b_low = b
    return dot(a_high, b_high, dims) + (dot(a_high, b_low, dims) + dot(a_low, b_high, dims))


def lanes(index, size):
    return pl.ds(pl.multiple_of(index * size, size), size)


def pack_kernel(size, pick_a, pick_b, *refs):
    ins, outs = refs[: 2 * SIDE], refs[2 * SIDE :]
    for half, pick in ((0, pick_a), (1, pick_b)):
        for far in range(SIDE):
            for near in range(SIDE):
                source = ins[half * SIDE + near]
                target = outs[half * SIDE + far]
                for k in range(SIDE):
                    for p in range(2):
                        block = pick[((far * SIDE + near) * SIDE + k) * 2 + p]
                        target[(near * SIDE + k) * 2 + p] = source[k, :, lanes(block, size)]


def unpack_kernel(size, pick_a, pick_b, *refs):
    ins, outs = refs[: 2 * SIDE], refs[2 * SIDE :]
    for out in outs:
        out[...] = jnp.zeros_like(out)
    for half, pick in ((0, pick_a), (1, pick_b)):
        for near in range(SIDE):
            target = outs[half * SIDE + near]
            for far in range(SIDE):
                source = ins[half * SIDE + far]
                for k in range(SIDE):
                    for p in range(2):
                        block = pick[((far * SIDE + near) * SIDE + k) * 2 + p]
                        target[k, :, lanes(block, size)] += source[(near * SIDE + k) * 2 + p]


def forward_kernel(
    groups, rows, at_a, at_b, info, tiles, scaled, root, q0, q1, q2, q3, q4, q5, q6, q7,
    o0, o1, o2, o3, blocks, total, sems,
):
    step = pl.program_id(0)
    parts = (q0, q1, q2, q3, q4, q5, q6, q7)
    per = q0.shape[0]

    @pl.when(step == 0)
    def _():
        copies = [
            pltpu.make_async_copy(
                part, blocks.at[i // SIDE, pl.ds((i % SIDE) * per, per)], sems.at[i]
            )
            for i, part in enumerate(parts)
        ]
        for copy in copies:
            copy.start()
        total[...] = jnp.zeros_like(total)
        for copy in copies:
            copy.wait()

    first = step * GROUP

    @pl.when(first < info[0])
    def _():
        sums = []
        for u in range(GROUP):
            block = jnp.concatenate([blocks[0, at_a[first + u]], blocks[1, at_b[first + u]]], 0)
            adjacency = tiles[u].astype(F32).astype(BF16)
            both = dot(jnp.concatenate(halves(block), 0), adjacency, NT)
            width = block.shape[0]
            sums.append(both[:width] + both[width:])
        for u in range(GROUP):
            total[rows[first + u]] += sums[u]

    @pl.when(step == pl.num_programs(0) - 1)
    def _():
        size = total.shape[2]
        own = info[1]
        for k, out in enumerate((o0, o1, o2, o3)):
            for h in range(2):
                b = (own ^ k) * 2 + h
                scale = root[:, lanes(b, size)]
                value = (total[b] + scaled[:, lanes(b, size)]) * scale
                out[:, h * size : (h + 1) * size] = value


def dense_kernel(
    scale, info, a0, a1, a2, a3, c0, c1, c2, c3, weight,
    y0, y1, y2, y3, b0, b1, b2, b3, g0, g1, g2, g3, work, work2,
):
    own = info[1]
    part = a0.shape[0]
    rows = [pl.ds(pl.multiple_of((own ^ k) * part, part), part) for k in range(4)]
    for k, (a, c) in enumerate(zip((a0, a1, a2, a3), (c0, c1, c2, c3))):
        work[rows[k], :] = a[...]
        work2[rows[k], :] = c[...]
    agg = halves(work[...])
    w = halves(weight[...])
    preact = dot3(w, agg, TN)
    gate = jax.nn.sigmoid(preact)
    delta = halves(work2[...] * gate * (1.0 + preact * (1.0 - gate)))
    work[...] = preact * gate
    for k, out in enumerate((y0, y1, y2, y3)):
        out[...] = work[rows[k], :]
    work2[...] = dot3(w, delta, NN)
    for k, out in enumerate((b0, b1, b2, b3)):
        out[...] = work2[rows[k], :]
    work[...] = dot3(agg, delta, NT) * scale
    for k, out in enumerate((g0, g1, g2, g3)):
        out[...] = work[rows[k], :]


def backward_kernel(
    rows, at_a, at_b, info, tiles, root, inverse, i0, i1, i2, i3,
    direct, e0, e1, e2, e3, e4, e5, e6, e7, blocks, source, sems,
):
    step = pl.program_id(0)
    parts = (e0, e1, e2, e3, e4, e5, e6, e7)
    per = e0.shape[0]
    size = tiles.shape[2]
    width = i0.shape[0]

    @pl.when(step == 0)
    def _():
        blocks[...] = jnp.zeros_like(blocks)
        own = info[1]
        for k, piece in enumerate((i0, i1, i2, i3)):
            for h in range(2):
                b = (own ^ k) * 2 + h
                at = lanes(b, size)
                value = piece[:, h * size : (h + 1) * size]
                direct[:, at] = value * inverse[:, at]
                source[b] = jnp.concatenate(halves(value * root[:, at]), 0)

    first = step * GROUP

    @pl.when(first < info[0])
    def _():
        sums = []
        for u in range(GROUP):
            adjacency = tiles[u].astype(F32).astype(BF16)
            both = dot(source[rows[first + u]], adjacency, NN)
            sums.append(both[:width] + both[width:])
        for u in range(GROUP):
            blocks[0, at_a[first + u]] += sums[u][: width // 2]
            blocks[1, at_b[first + u]] += sums[u][width // 2 :]

    @pl.when(step == pl.num_programs(0) - 1)
    def _():
        copies = [
            pltpu.make_async_copy(
                blocks.at[i // SIDE, pl.ds((i % SIDE) * per, per)], part, sems.at[i]
            )
            for i, part in enumerate(parts)
        ]
        for copy in copies:
            copy.start()
        for copy in copies:
            copy.wait()


VMEM = pl.BlockSpec(memory_space=pltpu.VMEM)
SMEM = pl.BlockSpec(memory_space=pltpu.SMEM)
ANY = pl.BlockSpec(memory_space=pl.ANY)
LIMIT = 40 * 1024 * 1024


def params():
    return pltpu.CompilerParams(vmem_limit_bytes=LIMIT)


def struct(*shape):
    return jax.ShapeDtypeStruct(shape, F32)


def on_device(
    features,
    weight,
    cotangent,
    degrees,
    tiles,
    block_rows,
    block_source,
    block_slot,
    block_count,
    pair_blocks,
):
    nodes, width = features.shape
    slots, size = tiles.shape[0], tiles.shape[1]
    groups = nodes // size
    half = width // 2
    quarter = nodes // 4
    n_row = lax.axis_size("row")
    own = lax.axis_index("row")
    own_col = lax.axis_index("col")
    z, x, y = own // (SIDE * SIDE), own // SIDE % SIDE, own % SIDE
    box = jnp.arange(SIDE, dtype=jnp.int32)

    degree_f = degrees.astype(F32)[None, :]
    root = lax.rsqrt(degree_f)
    inverse = 1.0 / degree_f
    features_t = features.T
    cotangent_t = cotangent.T

    near_z = (z ^ box)[None, None, :]
    far, near = box[:, None, None], box[None, :, None]
    pick_a = pair_blocks[
        row_id(z, x, (y + far) % SIDE), row_id(near_z, (x - near) % SIDE, y)
    ].reshape(-1)
    pick_b = pair_blocks[
        row_id(z, (x + far) % SIDE, y), row_id(near_z, x, (y - near) % SIDE)
    ].reshape(-1)

    live = jnp.arange(slots, dtype=jnp.int32) < block_count[0]
    k = (block_source // (SIDE * SIDE)) ^ z
    dx = (x - block_source // SIDE) % SIDE
    dy = (y - block_source) % SIDE
    at_a = ((dy * SIDE + dx) * SIDE + k) * 2 + block_slot
    at_b = ((dx * SIDE + dy) * SIDE + k) * 2 + block_slot
    per = SIDE * SIDE * 2
    n_blocks = per * SIDE
    rows_forward = jnp.where(live, block_rows, groups)
    at_a_back = jnp.where(live, at_a, n_blocks)
    at_b_back = jnp.where(live, at_b, n_blocks)
    info = jnp.stack([block_count[0], own_col.astype(jnp.int32)])

    scaled = features_t * root
    stack = [scaled] + [swap_z(scaled, d) for d in range(1, SIDE)]
    stack_a = jnp.stack([s[:half] for s in stack])
    stack_b = jnp.stack([s[half:] for s in stack])
    near_a = [stack_a] + [shift_x(stack_a, d) for d in (1, 2, 3)]
    near_b = [stack_b] + [shift_y(stack_b, d) for d in (1, 2, 3)]
    packed = pl.pallas_call(
        functools.partial(pack_kernel, size),
        out_shape=[struct(per, half, size)] * (2 * SIDE),
        in_specs=[SMEM] * 2 + [VMEM] * (2 * SIDE),
        out_specs=[VMEM] * (2 * SIDE),
        compiler_params=params(),
        name="pack",
    )(pick_a, pick_b, *near_a, *near_b)
    got_a = [packed[0]] + [shift_y(packed[d], d) for d in (1, 2, 3)]
    got_b = [packed[SIDE]] + [shift_x(packed[SIDE + d], d) for d in (1, 2, 3)]

    whole = lambda shape: pl.BlockSpec(shape, lambda i, *_: (0,) * len(shape))
    tile_spec = pl.BlockSpec((GROUP, size, size), lambda i, *_: (i, 0, 0))
    agg = pl.pallas_call(
        functools.partial(forward_kernel, groups),
        out_shape=[struct(width, quarter)] * 4,
        grid_spec=pltpu.PrefetchScalarGridSpec(
            num_scalar_prefetch=4,
            grid=(slots // GROUP,),
            in_specs=[tile_spec, whole((width, nodes)), whole((1, nodes))] + [ANY] * (2 * SIDE),
            out_specs=[whole((width, quarter))] * 4,
            scratch_shapes=[
                pltpu.VMEM((2, n_blocks, half, size), F32),
                pltpu.VMEM((groups + 1, width, size), F32),
                pltpu.SemaphoreType.DMA((2 * SIDE,)),
            ],
        ),
        compiler_params=params(),
        name="forward",
    )(rows_forward, at_a, at_b, info, tiles, scaled, root, *got_a, *got_b)

    def piece(value, d):
        return lax.dynamic_slice_in_dim(value, (own_col ^ d) * quarter, quarter, 1)

    def exchange(pieces):
        return [pieces[0]] + [swap_col(pieces[d], d) for d in (1, 2, 3)]

    cot = exchange([piece(cotangent_t, d) for d in range(4)])
    agg = exchange(agg)
    dense = pl.pallas_call(
        functools.partial(dense_kernel, (n_row * nodes) ** (-0.5)),
        out_shape=[struct(width, quarter)] * 8 + [struct(width, 4 * width)] * 4,
        in_specs=[SMEM] + [VMEM] * 9,
        out_specs=[VMEM] * 12,
        scratch_shapes=[
            pltpu.VMEM((4 * width, quarter), F32),
            pltpu.VMEM((4 * width, quarter), F32),
        ],
        compiler_params=params(),
        name="dense",
    )(info, *agg, *cot, weight)
    back = exchange(dense[4:8])

    direct, *sent = pl.pallas_call(
        backward_kernel,
        out_shape=[struct(width, nodes)] + [struct(per, half, size)] * (2 * SIDE),
        grid_spec=pltpu.PrefetchScalarGridSpec(
            num_scalar_prefetch=4,
            grid=(slots // GROUP,),
            in_specs=[tile_spec, whole((1, nodes)), whole((1, nodes))]
            + [whole((width, quarter))] * 4,
            out_specs=[whole((width, nodes))] + [ANY] * (2 * SIDE),
            scratch_shapes=[
                pltpu.VMEM((2, n_blocks + 1, half, size), F32),
                pltpu.VMEM((groups, 2 * width, size), BF16),
                pltpu.SemaphoreType.DMA((2 * SIDE,)),
            ],
        ),
        compiler_params=params(),
        name="backward",
    )(block_rows, at_a_back, at_b_back, info, tiles, root, inverse, *back)

    home_a = [sent[0]] + [shift_y(sent[d], -d) for d in (1, 2, 3)]
    home_b = [sent[SIDE]] + [shift_x(sent[SIDE + d], -d) for d in (1, 2, 3)]
    summed = pl.pallas_call(
        functools.partial(unpack_kernel, size),
        out_shape=[struct(SIDE, half, nodes)] * (2 * SIDE),
        in_specs=[SMEM] * 2 + [VMEM] * (2 * SIDE),
        out_specs=[VMEM] * (2 * SIDE),
        compiler_params=params(),
        name="unpack",
    )(pick_a, pick_b, *home_a, *home_b)
    sum_a = summed[0] + shift_x(summed[1], -1) + shift_x(summed[2], -2) + shift_x(summed[3], -3)
    sum_b = summed[4] + shift_y(summed[5], -1) + shift_y(summed[6], -2) + shift_y(summed[7], -3)
    ends = [jnp.concatenate([sum_a[d], sum_b[d]], 0) for d in range(SIDE)]
    summed_back = ends[0] + swap_z(ends[1], 1) + swap_z(ends[2], 2) + swap_z(ends[3], 3)
    h_grad = (root * summed_back + direct).T

    out = exchange(dense[0:4])
    output = jnp.zeros((width, nodes), F32)
    for d in range(4):
        output = lax.dynamic_update_slice_in_dim(output, out[d], (own_col ^ d) * quarter, 1)

    grad = sum(exchange(dense[8:12]))
    for move in (shift_y, shift_x, swap_z):
        grad = grad + move(grad, 1) + move(grad, 2) + move(grad, 3)
    return (output.T, h_grad, grad)


def solution(mesh):
    in_specs = (
        P("row", "col"),
        P(),
        P("row", "col"),
        P("row"),
        P("row", None, None),
        P("row"),
        P("row"),
        P("row"),
        P("row"),
        P(),
    )
    out_specs = (P("row", "col"), P("row", "col"), P("col", None))
    return jax.shard_map(
        on_device, mesh=mesh, in_specs=in_specs, out_specs=out_specs, check_vma=False
    )
```

```python
import functools

import jax
import jax.numpy as jnp
from jax import lax
from jax.experimental import pallas as pl
from jax.experimental.pallas import tpu as pltpu
from jax.sharding import PartitionSpec as P

SIDE = 4
RB = 8
GROUP = 8
CUTS = 4
PER = SIDE * SIDE * 2
F32 = jnp.float32
BF16 = jnp.bfloat16
NT = (((1,), (1,)), ((), ()))
NN = (((1,), (0,)), ((), ()))
TN = (((0,), (0,)), ((), ()))


def row_id(z, x, y):
    return z * SIDE * SIDE + x * SIDE + y


def shift(value, du, dv):
    pairs = []
    for row in range(SIDE**3):
        z, x, y = row // (SIDE * SIDE), row // SIDE % SIDE, row % SIDE
        for col in range(4):
            dx, dy = (dv, du) if col % 2 else (du, dv)
            pairs.append((row * 4 + col, row_id(z, (x + dx) % SIDE, (y + dy) % SIDE) * 4 + col))
    return lax.ppermute(value, ("row", "col"), pairs)


def swap_z(value, k):
    return lax.ppermute(value, "row", [(r, r ^ (k * SIDE * SIDE)) for r in range(SIDE**3)])


def swap_col(value, k):
    return lax.ppermute(value, "col", [(c, c ^ k) for c in range(4)])


def halves(value):
    high = value.astype(BF16)
    return high, (value - high.astype(F32)).astype(BF16)


def dot(a, b, dims):
    return lax.dot_general(a, b, dims, preferred_element_type=F32)


def dot3(a, b, dims):
    a_high, a_low = a
    b_high, b_low = b
    return dot(a_high, b_high, dims) + (dot(a_high, b_low, dims) + dot(a_low, b_high, dims))


def lanes(index, size):
    return pl.ds(pl.multiple_of(index * size, size), size)


def fetch(sources, targets, sems):
    copies = [
        pltpu.make_async_copy(source, target, sems.at[i])
        for i, (source, target) in enumerate(zip(sources, targets))
    ]
    for copy in copies:
        copy.start()
    return copies


def wait(copies):
    for copy in copies:
        copy.wait()


def convert_kernel(tiles, out, held, built, in_sems, out_sems):
    n = in_sems.shape[0]
    span = tiles.shape[0] // n
    cuts = [pl.ds(i * span, span) for i in range(n)]
    loads = fetch([tiles.at[c] for c in cuts], [held.at[c] for c in cuts], in_sems)
    copies = []
    for i, cut in enumerate(cuts):
        loads[i].wait()

        def one(t, carry):
            built[t] = held[t].astype(F32).astype(BF16)
            return carry

        lax.fori_loop(i * span, (i + 1) * span, one, 0, unroll=2)
        copy = pltpu.make_async_copy(built.at[cut], out.at[cut], out_sems.at[i])
        copy.start()
        copies.append(copy)
    wait(copies)


def pack_kernel(pick, *refs):
    n = SIDE
    ins, outs, (held, built, in_sems, out_sems) = refs[:n], refs[n : 2 * n], refs[2 * n :]
    wait(fetch(ins, [held.at[i] for i in range(n)], in_sems))
    copies = []
    for far in (2, 1, 3, 0):
        for near in range(SIDE):
            for k in range(SIDE):
                for p in range(2):
                    block = pick[((far * SIDE + near) * SIDE + k) * 2 + p]
                    built[far, (near * SIDE + k) * 2 + p] = held[near, k * RB + block]
        copy = pltpu.make_async_copy(built.at[far], outs[far], out_sems.at[far])
        copy.start()
        copies.append(copy)
    wait(copies)


def unpack_kernel(pick, *refs):
    n = SIDE
    ins, outs, (held, built, in_sems, out_sems) = refs[:n], refs[n : 2 * n], refs[2 * n :]
    loads = fetch(ins, [held.at[i] for i in range(n)], in_sems)
    built[...] = jnp.zeros_like(built)
    wait(loads)
    tail = (held[0, PER:] + held[1, PER:]) + (held[2, PER:] + held[3, PER:])
    copies = []
    for near in (2, 1, 3, 0):
        for far in range(SIDE):
            for k in range(SIDE):
                for p in range(2):
                    block = pick[((far * SIDE + near) * SIDE + k) * 2 + p]
                    built[near, k * RB + block] += held[far, (near * SIDE + k) * 2 + p]
        built[near, PER:] = tail
        copy = pltpu.make_async_copy(built.at[near], outs[near], out_sems.at[near])
        copy.start()
        copies.append(copy)
    wait(copies)


def join_kernel(*refs):
    n = SIDE
    ins, outs, (held, built, in_sems, out_sems) = refs[:n], refs[n : 2 * n], refs[2 * n :]
    wait(fetch(ins, [held.at[i] for i in range(n)], in_sems))
    copies = []
    for k in (2, 3, 1, 0):
        for target, source in ((pl.ds(0, RB), pl.ds(k * RB, RB)), (pl.ds(RB, 2), pl.ds(PER, 2))):
            built[k, target] = (held[0, source] + held[1, source]) + (
                held[2, source] + held[3, source]
            )
        copy = pltpu.make_async_copy(built.at[k], outs[k], out_sems.at[k])
        copy.start()
        copies.append(copy)
    wait(copies)


def run_groups(group, count, span, tile_loads):
    groups = (count + GROUP - 1) // GROUP
    step = span // GROUP
    for i, load in enumerate(tile_loads):
        load.wait()
        lax.fori_loop(jnp.minimum(i * step, groups), jnp.minimum((i + 1) * step, groups), group, 0)


def forward_kernel(
    rows, at, info, scaled, root, tiles, q0, q1, q2, q3,
    o0, o1, o2, o3, held, blocks, total, tile_sems, sems,
):
    span = tiles.shape[0] // CUTS
    cuts = [pl.ds(i * span, span) for i in range(CUTS)]
    loads = fetch((q0, q1, q2, q3), [blocks.at[pl.ds(i * PER, PER)] for i in range(SIDE)], sems)
    tile_loads = fetch([tiles.at[c] for c in cuts], [held.at[c] for c in cuts], tile_sems)
    total[...] = jnp.zeros_like(total)
    wait(loads)
    width = total.shape[1]

    def group(g, carry):
        first = g * GROUP
        sums = []
        for u in range(GROUP):
            pair = jnp.concatenate(halves(blocks[at[first + u]]), 0)
            both = dot(pair, held[first + u], NT)
            sums.append(both[:width] + both[width:])
        for u in range(GROUP):
            total[rows[first + u]] += sums[u]
        return carry

    run_groups(group, info[0], span, tile_loads)
    size = total.shape[2]
    own = info[1]
    for k, out in enumerate((o0, o1, o2, o3)):
        for h in range(2):
            b = (own ^ k) * 2 + h
            span = lanes(b, size)
            out[:, h * size : (h + 1) * size] = (total[b] + scaled[:, span]) * root[:, span]


def dense_kernel(
    scale, info, a0, a1, a2, a3, c0, c1, c2, c3, weight,
    b0, b1, b2, b3, y0, y1, y2, y3, work, work2,
):
    own = info[1]
    part = a0.shape[0]
    rows = [pl.ds(pl.multiple_of((own ^ k) * part, part), part) for k in range(4)]
    for k, (a, c) in enumerate(zip((a0, a1, a2, a3), (c0, c1, c2, c3))):
        work[rows[k], :] = a[...]
        work2[rows[k], :] = c[...]
    agg = halves(work[...])
    w = halves(weight[...])
    preact = dot3(w, agg, TN)
    gate = jax.nn.sigmoid(preact)
    delta = halves(work2[...] * gate * (1.0 + preact * (1.0 - gate)))
    work[...] = preact * gate
    for k, out in enumerate((y0, y1, y2, y3)):
        out[...] = work[rows[k], :]
    work2[...] = dot3(w, delta, NN)
    work[...] = dot3(agg, delta, NT) * scale
    for k, out in enumerate((b0, b1, b2, b3)):
        out[:part, :] = work2[rows[k], :]
        out[part:, :] = work[rows[k], :]


def backward_kernel(
    rows, at, info, root, inverse, i0, i1, i2, i3, tiles,
    direct, e0, e1, e2, e3, held, blocks, source, tail, tile_sems, sems, tail_sems,
):
    parts = (e0, e1, e2, e3)
    size = tiles.shape[2]
    width = i0.shape[0] // 2
    span = tiles.shape[0] // CUTS
    cuts = [pl.ds(i * span, span) for i in range(CUTS)]
    tile_loads = fetch([tiles.at[c] for c in cuts], [held.at[c] for c in cuts], tile_sems)
    for h in range(2):
        cols = slice(h * size, (h + 1) * size)
        tail[h] = (i0[width:, cols] + i1[width:, cols]) + (i2[width:, cols] + i3[width:, cols])
    tails = fetch([tail] * SIDE, [part.at[pl.ds(PER, 2)] for part in parts], tail_sems)
    blocks[...] = jnp.zeros_like(blocks)
    own = info[1]
    for k, piece in enumerate((i0, i1, i2, i3)):
        for h in range(2):
            b = (own ^ k) * 2 + h
            where = lanes(b, size)
            value = piece[:width, h * size : (h + 1) * size]
            direct[:, where] = value * inverse[:, where]
            source[b] = jnp.concatenate(halves(value * root[:, where]), 0)

    def group(g, carry):
        first = g * GROUP
        sums = []
        for u in range(GROUP):
            both = dot(source[rows[first + u]], held[first + u], NN)
            sums.append(both[:width] + both[width:])
        for u in range(GROUP):
            blocks[at[first + u]] += sums[u]
        return carry

    run_groups(group, info[0], span, tile_loads)
    sent = fetch(
        [blocks.at[pl.ds(i * PER, PER)] for i in range(SIDE)],
        [part.at[pl.ds(0, PER)] for part in parts],
        sems,
    )
    wait(sent)
    wait(tails)


VMEM = pl.BlockSpec(memory_space=pltpu.VMEM)
SMEM = pl.BlockSpec(memory_space=pltpu.SMEM)
HBM = pl.BlockSpec(memory_space=pltpu.HBM)
LIMIT = 40 * 1024 * 1024
DMA = pltpu.SemaphoreType.DMA


def struct(*shape):
    return jax.ShapeDtypeStruct(shape, F32)


def call(kernel, name, out_shape, in_specs, out_specs, scratch, nbytes=1 << 22):
    return pl.pallas_call(
        kernel,
        out_shape=out_shape,
        in_specs=in_specs,
        out_specs=out_specs,
        scratch_shapes=scratch,
        compiler_params=pltpu.CompilerParams(vmem_limit_bytes=LIMIT),
        cost_estimate=pl.CostEstimate(flops=0, bytes_accessed=nbytes, transcendentals=0),
        name=name,
    )


def on_device(
    features,
    weight,
    cotangent,
    degrees,
    tiles,
    block_rows,
    block_source,
    block_slot,
    block_count,
    pair_blocks,
):
    nodes, width = features.shape
    slots, size = tiles.shape[0], tiles.shape[1]
    quarter = nodes // 4
    n_row = lax.axis_size("row")
    own = lax.axis_index("row")
    own_col = lax.axis_index("col")
    turned = own_col % 2 == 1

    def place(row):
        x, y = row // SIDE % SIDE, row % SIDE
        return row // (SIDE * SIDE), jnp.where(turned, y, x), jnp.where(turned, x, y)

    def row_at(z, u, v):
        return jnp.where(turned, row_id(z, v % SIDE, u % SIDE), row_id(z, u % SIDE, v % SIDE))

    z, u, v = place(own)
    box = jnp.arange(SIDE, dtype=jnp.int32)

    degree_f = degrees.astype(F32)[None, :]
    root = lax.rsqrt(degree_f)
    inverse = 1.0 / degree_f
    features_t = features.T
    cotangent_t = cotangent.T

    far, near, deep = box[:, None, None], box[None, :, None], box[None, None, :]
    pick = pair_blocks[row_at(z, u, v + far), row_at(z ^ deep, u - near, v)].reshape(-1)

    live = jnp.arange(slots, dtype=jnp.int32) < block_count[0]
    from_z, from_u, from_v = place(block_source)
    at = (v - from_v) % SIDE * SIDE + (u - from_u) % SIDE
    at = (at * SIDE + (from_z ^ z)) * 2 + block_slot
    n_blocks = PER * SIDE
    rows_forward = jnp.where(live, block_rows, RB)
    at_back = jnp.where(live, at, n_blocks)
    info = jnp.stack([block_count[0], own_col.astype(jnp.int32)])

    scaled = features_t * root
    blocked = scaled.reshape(width, RB, size).transpose(1, 0, 2)
    stack = [blocked] + [swap_z(blocked, d) for d in range(1, SIDE)]
    adjacency = call(
        convert_kernel,
        "convert",
        jax.ShapeDtypeStruct(tiles.shape, BF16),
        [HBM],
        HBM,
        [pltpu.VMEM(tiles.shape, jnp.int32), pltpu.VMEM(tiles.shape, BF16), DMA((8,)), DMA((8,))],
        nbytes=12 << 20,
    )(tiles)
    stack, adjacency, pick = lax.optimization_barrier((stack, adjacency, pick))
    stack = jnp.concatenate(stack)
    arrived = [stack] + [shift(stack, d, 0) for d in (1, 2, 3)]
    shape = (PER, width, size)
    packed = call(
        pack_kernel,
        "pack",
        [struct(*shape)] * SIDE,
        [SMEM] + [HBM] * SIDE,
        [HBM] * SIDE,
        [pltpu.VMEM((SIDE,) + shape, F32)] * 2 + [DMA((SIDE,))] * 2,
        nbytes=8 << 20,
    )(pick, *arrived)

    def piece(value, d):
        return lax.dynamic_slice_in_dim(value, (own_col ^ d) * quarter, quarter, 1)

    def exchange(pieces):
        return [pieces[0]] + [swap_col(pieces[d], d) for d in (1, 2, 3)]

    cot = [piece(cotangent_t, d) for d in range(4)]
    cot, packed = lax.optimization_barrier((cot, packed))
    got = [packed[0]] + [shift(packed[d], 0, d) for d in (1, 2, 3)]
    cot = exchange(cot)
    got, cot = lax.optimization_barrier((got, cot))
    agg = call(
        forward_kernel,
        "forward",
        [struct(width, quarter)] * 4,
        [SMEM] * 3 + [VMEM] * 2 + [HBM] * (SIDE + 1),
        [VMEM] * 4,
        [
            pltpu.VMEM(tiles.shape, BF16),
            pltpu.VMEM((n_blocks, width, size), F32),
            pltpu.VMEM((RB + 1, width, size), F32),
            DMA((CUTS,)),
            DMA((SIDE,)),
        ],
        nbytes=16 << 20,
    )(rows_forward, at, info, scaled, root, adjacency, *got)
    agg = exchange(agg)
    dense = call(
        functools.partial(dense_kernel, (n_row * nodes) ** (-0.5)),
        "dense",
        [struct(2 * width, quarter)] * 4 + [struct(width, quarter)] * 4,
        [SMEM] + [VMEM] * 9,
        [VMEM] * 8,
        [pltpu.VMEM((4 * width, quarter), F32), pltpu.VMEM((4 * width, quarter), F32)],
    )(info, *agg, *cot, weight)
    back = exchange(dense[:4])

    shape = (PER + 2, width, size)
    direct, *sent = call(
        backward_kernel,
        "backward",
        [struct(width, nodes)] + [struct(*shape)] * SIDE,
        [SMEM] * 3 + [VMEM] * 6 + [HBM],
        [VMEM] + [HBM] * SIDE,
        [
            pltpu.VMEM(tiles.shape, BF16),
            pltpu.VMEM((n_blocks + 1, width, size), F32),
            pltpu.VMEM((RB, 2 * width, size), BF16),
            pltpu.VMEM((2, width, size), F32),
            DMA((CUTS,)),
            DMA((SIDE,)),
            DMA((SIDE,)),
        ],
        nbytes=16 << 20,
    )(block_rows, at_back, info, root, inverse, *back, adjacency)

    sent, out = lax.optimization_barrier((sent, dense[4:]))
    home = [sent[0]] + [shift(sent[d], 0, -d) for d in (1, 2, 3)]
    out = exchange(out)
    home, out = lax.optimization_barrier((home, out))
    summed = call(
        unpack_kernel,
        "unpack",
        [struct(*shape)] * SIDE,
        [SMEM] + [HBM] * SIDE,
        [HBM] * SIDE,
        [pltpu.VMEM((SIDE,) + shape, F32)] * 2 + [DMA((SIDE,))] * 2,
        nbytes=8 << 20,
    )(pick, *home)
    arrived = [summed[0]] + [shift(summed[d], -d, 0) for d in (1, 2, 3)]
    ends = call(
        join_kernel,
        "join",
        [struct(RB + 2, width, size)] * SIDE,
        [HBM] * SIDE,
        [HBM] * SIDE,
        [pltpu.VMEM((SIDE,) + shape, F32), pltpu.VMEM((SIDE, RB + 2, width, size), F32)]
        + [DMA((SIDE,))] * 2,
        nbytes=8 << 20,
    )(*arrived)
    total = ends[0] + swap_z(ends[1], 1) + swap_z(ends[2], 2) + swap_z(ends[3], 3)
    summed_back = total[:RB].transpose(1, 0, 2).reshape(width, nodes)
    h_grad = (root * summed_back + direct).T
    grad = total[RB:].transpose(1, 0, 2).reshape(width, 4 * width)

    output = jnp.zeros((width, nodes), F32)
    for d in range(4):
        output = lax.dynamic_update_slice_in_dim(output, out[d], (own_col ^ d) * quarter, 1)
    return (output.T, h_grad, grad)


def solution(mesh):
    in_specs = (
        P("row", "col"),
        P(),
        P("row", "col"),
        P("row"),
        P("row", None, None),
        P("row"),
        P("row"),
        P("row"),
        P("row"),
        P(),
    )
    out_specs = (P("row", "col"), P("row", "col"), P("col", None))
    return jax.shard_map(
        on_device, mesh=mesh, in_specs=in_specs, out_specs=out_specs, check_vma=False
    )
```

```python
import functools

import jax
import jax.numpy as jnp
from jax import lax
from jax.experimental import pallas as pl
from jax.experimental.pallas import tpu as pltpu
from jax.sharding import PartitionSpec as P

SIDE = 4
RB = 8
GROUP = 8
CUTS = 4
PER = SIDE * SIDE * 2
F32 = jnp.float32
BF16 = jnp.bfloat16
NT = (((1,), (1,)), ((), ()))
NN = (((1,), (0,)), ((), ()))
TN = (((0,), (0,)), ((), ()))


def row_id(z, x, y):
    return z * SIDE * SIDE + x * SIDE + y


def shift(value, du, dv):
    pairs = []
    for row in range(SIDE**3):
        z, x, y = row // (SIDE * SIDE), row // SIDE % SIDE, row % SIDE
        for col in range(4):
            dx, dy = (dv, du) if col % 2 else (du, dv)
            pairs.append((row * 4 + col, row_id(z, (x + dx) % SIDE, (y + dy) % SIDE) * 4 + col))
    return lax.ppermute(value, ("row", "col"), pairs)


def swap_z(value, k):
    return lax.ppermute(value, "row", [(r, r ^ (k * SIDE * SIDE)) for r in range(SIDE**3)])


def swap_col(value, k):
    return lax.ppermute(value, "col", [(c, c ^ k) for c in range(4)])


def halves(value):
    high = value.astype(BF16)
    return high, (value - high.astype(F32)).astype(BF16)


def dot(a, b, dims):
    return lax.dot_general(a, b, dims, preferred_element_type=F32)


def dot3(a, b, dims):
    a_high, a_low = a
    b_high, b_low = b
    return dot(a_high, b_high, dims) + (dot(a_high, b_low, dims) + dot(a_low, b_high, dims))


def lanes(index, size):
    return pl.ds(pl.multiple_of(index * size, size), size)


def fetch(sources, targets, sems):
    copies = [
        pltpu.make_async_copy(source, target, sems.at[i])
        for i, (source, target) in enumerate(zip(sources, targets))
    ]
    for copy in copies:
        copy.start()
    return copies


def wait(copies):
    for copy in copies:
        copy.wait()


def convert_kernel(tiles, out, held, built, in_sems, out_sems):
    n = in_sems.shape[0]
    span = tiles.shape[0] // n
    cuts = [pl.ds(i * span, span) for i in range(n)]
    loads = fetch([tiles.at[c] for c in cuts], [held.at[c] for c in cuts], in_sems)
    copies = []
    for i, cut in enumerate(cuts):
        loads[i].wait()

        def one(t, carry):
            built[t] = held[t].astype(F32).astype(BF16)
            return carry

        lax.fori_loop(i * span, (i + 1) * span, one, 0, unroll=2)
        copy = pltpu.make_async_copy(built.at[cut], out.at[cut], out_sems.at[i])
        copy.start()
        copies.append(copy)
    wait(copies)


SPANS = ((0, RB), (RB, RB), (2 * RB, 2 * RB))


def pack_kernel(pick, *refs):
    n = SIDE * len(SPANS)
    ins, outs = refs[:n], refs[n : n + SIDE]
    held, built, in_sems, out_sems = refs[n + SIDE :]
    spots = [held.at[near, pl.ds(*span)] for span in SPANS for near in range(SIDE)]
    wait(fetch(ins, spots, in_sems))
    copies = []
    for far in (2, 3, 1, 0):
        for near in range(SIDE):
            for k in range(SIDE):
                for p in range(2):
                    at = (near * SIDE + k) * 2 + p
                    built[far, at] = held[near, k * RB + pick[far * PER + at]]
        copy = pltpu.make_async_copy(built.at[far], outs[far], out_sems.at[far])
        copy.start()
        copies.append(copy)
    wait(copies)


def unpack_kernel(pick, *refs):
    n = SIDE * len(SPANS)
    ins, outs = refs[:SIDE], refs[SIDE : SIDE + n]
    held, built, in_sems, out_sems = refs[SIDE + n :]
    loads = fetch(ins, [held.at[i] for i in range(SIDE)], in_sems)
    built[...] = jnp.zeros_like(built)
    wait(loads)
    tail = (held[0, PER:] + held[1, PER:]) + (held[2, PER:] + held[3, PER:])
    copies = []
    for part in (2, 1, 0):
        start, size = SPANS[part]
        for near in (1, 2, 3, 0):
            for k in range(start // RB, (start + size) // RB):
                for far in range(SIDE):
                    for p in range(2):
                        at = (near * SIDE + k) * 2 + p
                        built[near, k * RB + pick[far * PER + at]] += held[far, at]
            if part == 2:
                built[near, PER:] = tail
            message = part * SIDE + near
            copy = pltpu.make_async_copy(
                built.at[near, pl.ds(start, size + 2 * (part == 2))],
                outs[message],
                out_sems.at[message],
            )
            copy.start()
            copies.append(copy)
    wait(copies)


def join_kernel(count, *refs):
    n = SIDE if count == 2 else SIDE + 1
    ins, outs = refs[:n], refs[n : n + count]
    held, built, in_sems, out_sems = refs[n + count :]
    targets = [held.at[i] for i in range(SIDE)]
    if count == 1:
        ins = ins[:SIDE] + (ins[SIDE].at[pl.ds(RB, 2)],)
        targets.append(built.at[0, pl.ds(RB, 2)])
    wait(fetch(ins, targets, in_sems))
    copies = []
    for k in range(count):
        spans = [(pl.ds(0, RB), pl.ds(k * RB, RB))]
        if count == 2:
            spans.append((pl.ds(RB, 2), pl.ds(2 * RB, 2)))
        for target, source in spans:
            built[k, target] = (held[0, source] + held[1, source]) + (
                held[2, source] + held[3, source]
            )
        copy = pltpu.make_async_copy(built.at[k], outs[k], out_sems.at[k])
        copy.start()
        copies.append(copy)
    wait(copies)


def run_groups(group, count, span, tile_loads):
    groups = (count + GROUP - 1) // GROUP
    step = span // GROUP
    for i, load in enumerate(tile_loads):
        load.wait()
        lax.fori_loop(jnp.minimum(i * step, groups), jnp.minimum((i + 1) * step, groups), group, 0)


def forward_kernel(
    rows, at, info, scaled, root, tiles, q0, q1, q2, q3,
    o0, o1, o2, o3, held, blocks, total, tile_sems, sems,
):
    span = tiles.shape[0] // CUTS
    cuts = [pl.ds(i * span, span) for i in range(CUTS)]
    parts = (q0, q1, q2, q3)
    loads = fetch(parts, [blocks.at[pl.ds(i * PER, PER)] for i in range(SIDE)], sems)
    tile_loads = fetch([tiles.at[c] for c in cuts], [held.at[c] for c in cuts], tile_sems)
    total[...] = jnp.zeros_like(total)
    wait(loads)
    width = total.shape[1]

    def group(g, carry):
        first = g * GROUP
        sums = []
        for u in range(GROUP):
            pair = jnp.concatenate(halves(blocks[at[first + u]]), 0)
            both = dot(pair, held[first + u], NT)
            sums.append(both[:width] + both[width:])
        for u in range(GROUP):
            total[rows[first + u]] += sums[u]
        return carry

    run_groups(group, info[0], span, tile_loads)
    size = total.shape[2]
    own = info[1]
    for k, out in enumerate((o0, o1, o2, o3)):
        for h in range(2):
            b = (own ^ k) * 2 + h
            span = lanes(b, size)
            out[:, h * size : (h + 1) * size] = (total[b] + scaled[:, span]) * root[:, span]


def dense_kernel(
    scale, info, a0, a1, a2, a3, c0, c1, c2, c3, weight,
    b0, b1, b2, b3, y0, y1, y2, y3, work, work2,
):
    own = info[1]
    part = a0.shape[0]
    rows = [pl.ds(pl.multiple_of((own ^ k) * part, part), part) for k in range(4)]
    for k, (a, c) in enumerate(zip((a0, a1, a2, a3), (c0, c1, c2, c3))):
        work[rows[k], :] = a[...]
        work2[rows[k], :] = c[...]
    agg = halves(work[...])
    w = halves(weight[...])
    preact = dot3(w, agg, TN)
    gate = jax.nn.sigmoid(preact)
    delta = halves(work2[...] * gate * (1.0 + preact * (1.0 - gate)))
    work[...] = preact * gate
    for k, out in enumerate((y0, y1, y2, y3)):
        out[...] = work[rows[k], :]
    work2[...] = dot3(w, delta, NN)
    work[...] = dot3(agg, delta, NT) * scale
    for k, out in enumerate((b0, b1, b2, b3)):
        out[:part, :] = work2[rows[k], :]
        out[part:, :] = work[rows[k], :]


def backward_kernel(
    rows, at, info, root, inverse, i0, i1, i2, i3, tiles,
    direct, e0, e1, e2, e3, held, blocks, source, tail, tile_sems, sems, tail_sems,
):
    parts = (e0, e1, e2, e3)
    size = tiles.shape[2]
    width = i0.shape[0] // 2
    span = tiles.shape[0] // CUTS
    cuts = [pl.ds(i * span, span) for i in range(CUTS)]
    tile_loads = fetch([tiles.at[c] for c in cuts], [held.at[c] for c in cuts], tile_sems)
    for h in range(2):
        cols = slice(h * size, (h + 1) * size)
        tail[h] = (i0[width:, cols] + i1[width:, cols]) + (i2[width:, cols] + i3[width:, cols])
    tails = fetch([tail] * SIDE, [part.at[pl.ds(PER, 2)] for part in parts], tail_sems)
    blocks[...] = jnp.zeros_like(blocks)
    own = info[1]
    for k, piece in enumerate((i0, i1, i2, i3)):
        for h in range(2):
            b = (own ^ k) * 2 + h
            where = lanes(b, size)
            value = piece[:width, h * size : (h + 1) * size]
            direct[:, where] = value * inverse[:, where]
            source[b] = jnp.concatenate(halves(value * root[:, where]), 0)

    def group(g, carry):
        first = g * GROUP
        sums = []
        for u in range(GROUP):
            both = dot(source[rows[first + u]], held[first + u], NN)
            sums.append(both[:width] + both[width:])
        for u in range(GROUP):
            blocks[at[first + u]] += sums[u]
        return carry

    run_groups(group, info[0], span, tile_loads)
    sent = fetch(
        [blocks.at[pl.ds(i * PER, PER)] for i in range(SIDE)],
        [part.at[pl.ds(0, PER)] for part in parts],
        sems,
    )
    wait(sent)
    wait(tails)


VMEM = pl.BlockSpec(memory_space=pltpu.VMEM)
SMEM = pl.BlockSpec(memory_space=pltpu.SMEM)
HBM = pl.BlockSpec(memory_space=pltpu.HBM)
LIMIT = 40 * 1024 * 1024
DMA = pltpu.SemaphoreType.DMA


def struct(*shape):
    return jax.ShapeDtypeStruct(shape, F32)


def call(kernel, name, out_shape, in_specs, out_specs, scratch, nbytes=1 << 22):
    return pl.pallas_call(
        kernel,
        out_shape=out_shape,
        in_specs=in_specs,
        out_specs=out_specs,
        scratch_shapes=scratch,
        compiler_params=pltpu.CompilerParams(vmem_limit_bytes=LIMIT),
        cost_estimate=pl.CostEstimate(flops=0, bytes_accessed=nbytes, transcendentals=0),
        name=name,
    )


def on_device(
    features,
    weight,
    cotangent,
    degrees,
    tiles,
    block_rows,
    block_source,
    block_slot,
    block_count,
    pair_blocks,
):
    nodes, width = features.shape
    slots, size = tiles.shape[0], tiles.shape[1]
    quarter = nodes // 4
    n_row = lax.axis_size("row")
    own = lax.axis_index("row")
    own_col = lax.axis_index("col")
    turned = own_col % 2 == 1

    def place(row):
        x, y = row // SIDE % SIDE, row % SIDE
        return row // (SIDE * SIDE), jnp.where(turned, y, x), jnp.where(turned, x, y)

    def row_at(z, u, v):
        return jnp.where(turned, row_id(z, v % SIDE, u % SIDE), row_id(z, u % SIDE, v % SIDE))

    z, u, v = place(own)
    box = jnp.arange(SIDE, dtype=jnp.int32)

    degree_f = degrees.astype(F32)[None, :]
    root = lax.rsqrt(degree_f)
    inverse = 1.0 / degree_f
    features_t = features.T
    cotangent_t = cotangent.T

    far, near, deep = box[:, None, None], box[None, :, None], box[None, None, :]
    pick = pair_blocks[row_at(z, u, v + far), row_at(z ^ deep, u - near, v)].reshape(-1)

    live = jnp.arange(slots, dtype=jnp.int32) < block_count[0]
    from_z, from_u, from_v = place(block_source)
    at = (v - from_v) % SIDE * SIDE + (u - from_u) % SIDE
    at = (at * SIDE + (from_z ^ z)) * 2 + block_slot
    n_blocks = PER * SIDE
    rows_forward = jnp.where(live, block_rows, RB)
    at_back = jnp.where(live, at, n_blocks)
    info = jnp.stack([block_count[0], own_col.astype(jnp.int32)])

    def piece(value, d):
        return lax.dynamic_slice_in_dim(value, (own_col ^ d) * quarter, quarter, 1)

    def exchange(pieces):
        return [pieces[0]] + [swap_col(pieces[d], d) for d in (1, 2, 3)]

    shape = (PER, width, size)
    longer = (PER + 2, width, size)
    lengths = [size + 2 * (i == 2) for i, (_, size) in enumerate(SPANS)]

    def spread(value):
        return [value] + [shift(value, d, 0) for d in (1, 2, 3)]

    def route(values):
        return [values[0]] + [shift(values[d], -d, 0) for d in (1, 2, 3)]

    def join(arrived, *more):
        count = 1 if more else 2
        return call(
            functools.partial(join_kernel, count),
            "join%d" % count,
            [struct(RB + 2, width, size)] * count,
            [HBM] * (SIDE + len(more)),
            [HBM] * count,
            [
                pltpu.VMEM((SIDE,) + arrived[0].shape, F32),
                pltpu.VMEM((count, RB + 2, width, size), F32),
                DMA((SIDE + 1,)),
                DMA((count,)),
            ],
        )(*arrived, *more)

    scaled = features_t * root
    blocked = scaled.reshape(width, RB, size).transpose(1, 0, 2)
    deep = [blocked] + [swap_z(blocked, d) for d in range(1, SIDE)]
    adjacency = call(
        convert_kernel,
        "convert",
        jax.ShapeDtypeStruct(tiles.shape, BF16),
        [HBM],
        HBM,
        [pltpu.VMEM(tiles.shape, jnp.int32), pltpu.VMEM(tiles.shape, BF16), DMA((8,)), DMA((8,))],
        nbytes=12 << 20,
    )(tiles)
    cot = [piece(cotangent_t, d) for d in range(4)]
    own_part = spread(blocked)
    next_part = spread(deep[1])
    own_part, next_part, far_deep, adjacency, pick, cot = lax.optimization_barrier(
        (own_part, next_part, deep[2:], adjacency, pick, cot)
    )
    far_part = spread(jnp.concatenate(far_deep))
    packed = call(
        pack_kernel,
        "pack",
        [struct(*shape)] * SIDE,
        [SMEM] + [HBM] * (3 * SIDE),
        [HBM] * SIDE,
        [
            pltpu.VMEM((SIDE,) + shape, F32),
            pltpu.VMEM((SIDE,) + shape, F32),
            DMA((3 * SIDE,)),
            DMA((SIDE,)),
        ],
        nbytes=8 << 20,
    )(pick, *own_part, *next_part, *far_part)
    cot, packed = lax.optimization_barrier((cot, packed))
    got = [packed[0]] + [shift(packed[d], 0, d) for d in (1, 2, 3)]
    cot = exchange(cot)
    got, cot = lax.optimization_barrier((got, cot))
    agg = call(
        forward_kernel,
        "forward",
        [struct(width, quarter)] * 4,
        [SMEM] * 3 + [VMEM] * 2 + [HBM] * (SIDE + 1),
        [VMEM] * 4,
        [
            pltpu.VMEM(tiles.shape, BF16),
            pltpu.VMEM((n_blocks, width, size), F32),
            pltpu.VMEM((RB + 1, width, size), F32),
            DMA((CUTS,)),
            DMA((SIDE,)),
        ],
        nbytes=16 << 20,
    )(rows_forward, at, info, scaled, root, adjacency, *got)
    agg = exchange(agg)
    dense = call(
        functools.partial(dense_kernel, (n_row * nodes) ** (-0.5)),
        "dense",
        [struct(2 * width, quarter)] * 4 + [struct(width, quarter)] * 4,
        [SMEM] + [VMEM] * 9,
        [VMEM] * 8,
        [pltpu.VMEM((4 * width, quarter), F32), pltpu.VMEM((4 * width, quarter), F32)],
    )(info, *agg, *cot, weight)
    back = exchange(dense[:4])

    direct, *sent = call(
        backward_kernel,
        "backward",
        [struct(width, nodes)] + [struct(*longer)] * SIDE,
        [SMEM] * 3 + [VMEM] * 6 + [HBM],
        [VMEM] + [HBM] * SIDE,
        [
            pltpu.VMEM(tiles.shape, BF16),
            pltpu.VMEM((n_blocks + 1, width, size), F32),
            pltpu.VMEM((RB, 2 * width, size), BF16),
            pltpu.VMEM((2, width, size), F32),
            DMA((CUTS,)),
            DMA((SIDE,)),
            DMA((SIDE,)),
        ],
        nbytes=16 << 20,
    )(block_rows, at_back, info, root, inverse, *back, adjacency)

    sent, out = lax.optimization_barrier((sent, dense[4:]))
    home = [sent[0]] + [shift(sent[d], 0, -d) for d in (1, 2, 3)]
    out = exchange(out)
    home, out = lax.optimization_barrier((home, out))
    summed = call(
        unpack_kernel,
        "unpack",
        [struct(length, width, size) for length in lengths for _ in range(SIDE)],
        [SMEM] + [HBM] * SIDE,
        [HBM] * (3 * SIDE),
        [
            pltpu.VMEM((SIDE,) + longer, F32),
            pltpu.VMEM((SIDE,) + longer, F32),
            DMA((SIDE,)),
            DMA((3 * SIDE,)),
        ],
        nbytes=8 << 20,
    )(pick, *home)
    own_part, next_part, far_part = summed[:SIDE], summed[SIDE : 2 * SIDE], summed[2 * SIDE :]
    far_part, next_part = lax.optimization_barrier((route(far_part), next_part))
    far_ends = join(far_part)
    next_part, own_part = lax.optimization_barrier((route(next_part), own_part))
    next_end = join(next_part, far_ends[0])[0]
    own_part = route(own_part)
    ends = [swap_z(next_end, 1), swap_z(far_ends[0], 2), swap_z(far_ends[1], 3)]
    total = (ends[0][:RB] + ends[1][:RB]) + ends[2][:RB]
    total += (own_part[0] + own_part[1]) + (own_part[2] + own_part[3])
    tail = (far_ends[0][RB:] + ends[0][RB:]) + (ends[1][RB:] + ends[2][RB:])
    summed_back = total.transpose(1, 0, 2).reshape(width, nodes)
    h_grad = (root * summed_back + direct).T
    grad = tail.transpose(1, 0, 2).reshape(width, 4 * width)

    output = jnp.zeros((width, nodes), F32)
    for d in range(4):
        output = lax.dynamic_update_slice_in_dim(output, out[d], (own_col ^ d) * quarter, 1)
    return (output.T, h_grad, grad)


def solution(mesh):
    in_specs = (
        P("row", "col"),
        P(),
        P("row", "col"),
        P("row"),
        P("row", None, None),
        P("row"),
        P("row"),
        P("row"),
        P("row"),
        P(),
    )
    out_specs = (P("row", "col"), P("row", "col"), P("col", None))
    return jax.shard_map(
        on_device, mesh=mesh, in_specs=in_specs, out_specs=out_specs, check_vma=False
    )
```

```python
import functools

import jax
import jax.numpy as jnp
from jax import lax
from jax.experimental import pallas as pl
from jax.experimental.pallas import tpu as pltpu
from jax.sharding import PartitionSpec as P

SIDE = 4
RB = 8
GROUP = 16
CUTS = 4
PER = SIDE * SIDE * 2
F32 = jnp.float32
BF16 = jnp.bfloat16
NT = (((1,), (1,)), ((), ()))
NN = (((1,), (0,)), ((), ()))
TN = (((0,), (0,)), ((), ()))


def row_id(z, x, y):
    return z * SIDE * SIDE + x * SIDE + y


def shift(value, du, dv):
    pairs = []
    for row in range(SIDE**3):
        z, x, y = row // (SIDE * SIDE), row // SIDE % SIDE, row % SIDE
        for col in range(4):
            dx, dy = (dv, du) if col % 2 else (du, dv)
            pairs.append((row * 4 + col, row_id(z, (x + dx) % SIDE, (y + dy) % SIDE) * 4 + col))
    return lax.ppermute(value, ("row", "col"), pairs)


def swap_z(value, k):
    return lax.ppermute(value, "row", [(r, r ^ (k * SIDE * SIDE)) for r in range(SIDE**3)])


def swap_col(value, k):
    return lax.ppermute(value, "col", [(c, c ^ k) for c in range(4)])


def halves(value):
    high = value.astype(BF16)
    return high, (value - high.astype(F32)).astype(BF16)


def dot(a, b, dims):
    return lax.dot_general(a, b, dims, preferred_element_type=F32)


def dot3(a, b, dims):
    a_high, a_low = a
    b_high, b_low = b
    return dot(a_high, b_high, dims) + (dot(a_high, b_low, dims) + dot(a_low, b_high, dims))


def lanes(index, size):
    return pl.ds(pl.multiple_of(index * size, size), size)


def fetch(sources, targets, sems):
    copies = [
        pltpu.make_async_copy(source, target, sems.at[i])
        for i, (source, target) in enumerate(zip(sources, targets))
    ]
    for copy in copies:
        copy.start()
    return copies


def wait(copies):
    for copy in copies:
        copy.wait()


def convert_kernel(tiles, out, held, built, in_sems, out_sems):
    n = in_sems.shape[0]
    span = tiles.shape[0] // n
    cuts = [pl.ds(i * span, span) for i in range(n)]
    loads = fetch([tiles.at[c] for c in cuts], [held.at[c] for c in cuts], in_sems)
    copies = []
    for i, cut in enumerate(cuts):
        loads[i].wait()

        def one(t, carry):
            built[t] = held[t].astype(F32).astype(BF16)
            return carry

        lax.fori_loop(i * span, (i + 1) * span, one, 0, unroll=2)
        copy = pltpu.make_async_copy(built.at[cut], out.at[cut], out_sems.at[i])
        copy.start()
        copies.append(copy)
    wait(copies)


SPANS = ((0, RB), (RB, RB), (2 * RB, 2 * RB))


def pack_kernel(pick, *refs):
    n = SIDE * len(SPANS)
    ins, outs = refs[:n], refs[n : n + SIDE]
    for far in range(SIDE):
        for near in range(SIDE):
            for k in range(SIDE):
                source, base = ins[min(k, 2) * SIDE + near], RB * (k == 3)
                for p in range(2):
                    at = (near * SIDE + k) * 2 + p
                    outs[far][at] = source[base + pick[far * PER + at]]


def unpack_kernel(pick, *refs):
    ins, outs = refs[:SIDE], refs[SIDE:]
    for out in outs:
        out[...] = jnp.zeros_like(out)
    tail = (ins[0][PER:] + ins[1][PER:]) + (ins[2][PER:] + ins[3][PER:])
    for near in range(SIDE):
        outs[2 * SIDE + near][2 * RB :] = tail
        for k in range(SIDE):
            target, base = outs[min(k, 2) * SIDE + near], RB * (k == 3)
            if k == 0 and near == 2:
                target, base = outs[SIDE + near], RB
            for far in range(SIDE):
                for p in range(2):
                    at = (near * SIDE + k) * 2 + p
                    target[base + pick[far * PER + at]] += ins[far][at]


def join_kernel(count, *refs):
    n = SIDE if count == 2 else SIDE + 1
    ins, outs = refs[:n], refs[n:]
    for k, out in enumerate(outs):
        spans = [(pl.ds(0, RB), pl.ds(k * RB, RB))]
        if count == 2:
            spans.append((pl.ds(RB, 2), pl.ds(2 * RB, 2)))
        else:
            out[RB:] = ins[SIDE][RB:]
        for target, source in spans:
            out[target] = (ins[0][source] + ins[1][source]) + (ins[2][source] + ins[3][source])


def run_groups(group, count, span, tile_loads):
    groups = (count + GROUP - 1) // GROUP
    step = span // GROUP
    for i, load in enumerate(tile_loads):
        load.wait()
        lax.fori_loop(jnp.minimum(i * step, groups), jnp.minimum((i + 1) * step, groups), group, 0)


def forward_kernel(
    rows, at, info, scaled, root, tiles, q0, q1, q2, q3,
    o0, o1, o2, o3, held, blocks, total, tile_sems, sems,
):
    span = tiles.shape[0] // CUTS
    cuts = [pl.ds(i * span, span) for i in range(CUTS)]
    parts = (q0, q1, q2, q3)
    loads = fetch(parts, [blocks.at[pl.ds(i * PER, PER)] for i in range(SIDE)], sems)
    tile_loads = fetch([tiles.at[c] for c in cuts], [held.at[c] for c in cuts], tile_sems)
    total[...] = jnp.zeros_like(total)
    wait(loads)
    width = total.shape[1]

    def group(g, carry):
        first = g * GROUP
        sums = []
        for u in range(GROUP):
            pair = jnp.concatenate(halves(blocks[at[first + u]]), 0)
            both = dot(pair, held[first + u], NT)
            sums.append(both[:width] + both[width:])
        for u in range(GROUP):
            total[rows[first + u]] += sums[u]
        return carry

    run_groups(group, info[0], span, tile_loads)
    size = total.shape[2]
    own = info[1]
    for k, out in enumerate((o0, o1, o2, o3)):
        for h in range(2):
            b = (own ^ k) * 2 + h
            span = lanes(b, size)
            out[:, h * size : (h + 1) * size] = (total[b] + scaled[:, span]) * root[:, span]


def dense_kernel(
    scale, info, a0, a1, a2, a3, c0, c1, c2, c3, weight,
    b0, b1, b2, b3, y0, y1, y2, y3, work, work2,
):
    own = info[1]
    part = a0.shape[0]
    rows = [pl.ds(pl.multiple_of((own ^ k) * part, part), part) for k in range(4)]
    for k, (a, c) in enumerate(zip((a0, a1, a2, a3), (c0, c1, c2, c3))):
        work[rows[k], :] = a[...]
        work2[rows[k], :] = c[...]
    agg = halves(work[...])
    w = halves(weight[...])
    preact = dot3(w, agg, TN)
    gate = jax.nn.sigmoid(preact)
    delta = halves(work2[...] * gate * (1.0 + preact * (1.0 - gate)))
    work[...] = preact * gate
    for k, out in enumerate((y0, y1, y2, y3)):
        out[...] = work[rows[k], :]
    work2[...] = dot3(w, delta, NN)
    work[...] = dot3(agg, delta, NT) * scale
    for k, out in enumerate((b0, b1, b2, b3)):
        out[:part, :] = work2[rows[k], :]
        out[part:, :] = work[rows[k], :]


def backward_kernel(
    rows, at, info, root, inverse, i0, i1, i2, i3, tiles,
    direct, e0, e1, e2, e3, held, blocks, source, tail, tile_sems, sems, tail_sems,
):
    parts = (e0, e1, e2, e3)
    size = tiles.shape[2]
    width = i0.shape[0] // 2
    span = tiles.shape[0] // CUTS
    cuts = [pl.ds(i * span, span) for i in range(CUTS)]
    tile_loads = fetch([tiles.at[c] for c in cuts], [held.at[c] for c in cuts], tile_sems)
    for h in range(2):
        cols = slice(h * size, (h + 1) * size)
        tail[h] = (i0[width:, cols] + i1[width:, cols]) + (i2[width:, cols] + i3[width:, cols])
    tails = fetch([tail] * SIDE, [part.at[pl.ds(PER, 2)] for part in parts], tail_sems)
    blocks[...] = jnp.zeros_like(blocks)
    own = info[1]
    for k, piece in enumerate((i0, i1, i2, i3)):
        for h in range(2):
            b = (own ^ k) * 2 + h
            where = lanes(b, size)
            value = piece[:width, h * size : (h + 1) * size]
            direct[:, where] = value * inverse[:, where]
            source[b] = jnp.concatenate(halves(value * root[:, where]), 0)

    def group(g, carry):
        first = g * GROUP
        sums = []
        for u in range(GROUP):
            both = dot(source[rows[first + u]], held[first + u], NN)
            sums.append(both[:width] + both[width:])
        for u in range(GROUP):
            blocks[at[first + u]] += sums[u]
        return carry

    run_groups(group, info[0], span, tile_loads)
    sent = fetch(
        [blocks.at[pl.ds(i * PER, PER)] for i in range(SIDE)],
        [part.at[pl.ds(0, PER)] for part in parts],
        sems,
    )
    wait(sent)
    wait(tails)


VMEM = pl.BlockSpec(memory_space=pltpu.VMEM)
SMEM = pl.BlockSpec(memory_space=pltpu.SMEM)
HBM = pl.BlockSpec(memory_space=pltpu.HBM)
LIMIT = 40 * 1024 * 1024
DMA = pltpu.SemaphoreType.DMA


def struct(*shape):
    return jax.ShapeDtypeStruct(shape, F32)


def call(kernel, name, out_shape, in_specs, out_specs, scratch, nbytes=1 << 22):
    return pl.pallas_call(
        kernel,
        out_shape=out_shape,
        in_specs=in_specs,
        out_specs=out_specs,
        scratch_shapes=scratch,
        compiler_params=pltpu.CompilerParams(vmem_limit_bytes=LIMIT),
        cost_estimate=pl.CostEstimate(flops=0, bytes_accessed=nbytes, transcendentals=0),
        name=name,
    )


def on_device(
    features,
    weight,
    cotangent,
    degrees,
    tiles,
    block_rows,
    block_source,
    block_slot,
    block_count,
    pair_blocks,
):
    nodes, width = features.shape
    slots, size = tiles.shape[0], tiles.shape[1]
    quarter = nodes // 4
    n_row = lax.axis_size("row")
    own = lax.axis_index("row")
    own_col = lax.axis_index("col")
    turned = own_col % 2 == 1

    def place(row):
        x, y = row // SIDE % SIDE, row % SIDE
        return row // (SIDE * SIDE), jnp.where(turned, y, x), jnp.where(turned, x, y)

    def row_at(z, u, v):
        return jnp.where(turned, row_id(z, v % SIDE, u % SIDE), row_id(z, u % SIDE, v % SIDE))

    z, u, v = place(own)
    box = jnp.arange(SIDE, dtype=jnp.int32)

    degree_f = degrees.astype(F32)[None, :]
    root = lax.rsqrt(degree_f)
    inverse = 1.0 / degree_f
    features_t = features.T
    cotangent_t = cotangent.T

    far, near, deep = box[:, None, None], box[None, :, None], box[None, None, :]
    pick = pair_blocks[row_at(z, u, v + far), row_at(z ^ deep, u - near, v)].reshape(-1)

    live = jnp.arange(slots, dtype=jnp.int32) < block_count[0]
    from_z, from_u, from_v = place(block_source)
    at = (v - from_v) % SIDE * SIDE + (u - from_u) % SIDE
    at = (at * SIDE + (from_z ^ z)) * 2 + block_slot
    n_blocks = PER * SIDE
    rows_forward = jnp.where(live, block_rows, RB)
    at_back = jnp.where(live, at, n_blocks)
    info = jnp.stack([block_count[0], own_col.astype(jnp.int32)])

    def piece(value, d):
        return lax.dynamic_slice_in_dim(value, (own_col ^ d) * quarter, quarter, 1)

    def exchange(pieces):
        return [pieces[0]] + [swap_col(pieces[d], d) for d in (1, 2, 3)]

    shape = (PER, width, size)
    longer = (PER + 2, width, size)
    lengths = [
        size + 2 * (part == 2) + RB * (part == 1 and near == 2)
        for part, (_, size) in enumerate(SPANS)
        for near in range(SIDE)
    ]

    def spread(value):
        return [value] + [shift(value, d, 0) for d in (1, 2, 3)]

    def route(values):
        return [values[0]] + [shift(values[d], -d, 0) for d in (1, 2, 3)]

    def join(arrived, *more):
        count = 1 if more else 2
        return call(
            functools.partial(join_kernel, count),
            "join%d" % count,
            [struct(RB + 2, width, size)] * count,
            [VMEM] * (SIDE + len(more)),
            [VMEM] * count,
            [],
        )(*arrived, *more)

    scaled = features_t * root
    blocked = scaled.reshape(width, RB, size).transpose(1, 0, 2)
    deep = [blocked] + [swap_z(blocked, d) for d in range(1, SIDE)]
    adjacency = call(
        convert_kernel,
        "convert",
        jax.ShapeDtypeStruct(tiles.shape, BF16),
        [HBM],
        HBM,
        [pltpu.VMEM(tiles.shape, jnp.int32), pltpu.VMEM(tiles.shape, BF16), DMA((8,)), DMA((8,))],
        nbytes=12 << 20,
    )(tiles)
    cot = [piece(cotangent_t, d) for d in range(4)]
    later, pick = lax.optimization_barrier((blocked, pick))
    own_part = spread(later)
    next_part = spread(deep[1])
    own_part, next_part, far_deep, adjacency, pick, cot = lax.optimization_barrier(
        (own_part, next_part, deep[2:], adjacency, pick, cot)
    )
    far_part = spread(jnp.concatenate(far_deep))
    packed = call(
        pack_kernel,
        "pack",
        [struct(*shape)] * SIDE,
        [SMEM] + [VMEM] * (3 * SIDE),
        [VMEM] * SIDE,
        [],
        nbytes=8 << 20,
    )(pick, *own_part, *next_part, *far_part)
    cot, packed = lax.optimization_barrier((cot, packed))
    got = [packed[0]] + [shift(packed[d], 0, d) for d in (1, 2, 3)]
    cot = exchange(cot)
    got, cot = lax.optimization_barrier((got, cot))
    agg = call(
        forward_kernel,
        "forward",
        [struct(width, quarter)] * 4,
        [SMEM] * 3 + [VMEM] * 2 + [HBM] * (SIDE + 1),
        [VMEM] * 4,
        [
            pltpu.VMEM(tiles.shape, BF16),
            pltpu.VMEM((n_blocks, width, size), F32),
            pltpu.VMEM((RB + 1, width, size), F32),
            DMA((CUTS,)),
            DMA((SIDE,)),
        ],
        nbytes=16 << 20,
    )(rows_forward, at, info, scaled, root, adjacency, *got)
    agg = exchange(agg)
    dense = call(
        functools.partial(dense_kernel, (n_row * nodes) ** (-0.5)),
        "dense",
        [struct(2 * width, quarter)] * 4 + [struct(width, quarter)] * 4,
        [SMEM] + [VMEM] * 9,
        [VMEM] * 8,
        [pltpu.VMEM((4 * width, quarter), F32), pltpu.VMEM((4 * width, quarter), F32)],
    )(info, *agg, *cot, weight)
    back = exchange(dense[:4])

    direct, *sent = call(
        backward_kernel,
        "backward",
        [struct(width, nodes)] + [struct(*longer)] * SIDE,
        [SMEM] * 3 + [VMEM] * 6 + [HBM],
        [VMEM] + [HBM] * SIDE,
        [
            pltpu.VMEM(tiles.shape, BF16),
            pltpu.VMEM((n_blocks + 1, width, size), F32),
            pltpu.VMEM((RB, 2 * width, size), BF16),
            pltpu.VMEM((2, width, size), F32),
            DMA((CUTS,)),
            DMA((SIDE,)),
            DMA((SIDE,)),
        ],
        nbytes=16 << 20,
    )(block_rows, at_back, info, root, inverse, *back, adjacency)

    sent, out = lax.optimization_barrier((sent, dense[4:]))
    home = [sent[0]] + [shift(sent[d], 0, -d) for d in (1, 2, 3)]
    out = exchange(out)
    home, out = lax.optimization_barrier((home, out))
    summed = call(
        unpack_kernel,
        "unpack",
        [struct(length, width, size) for length in lengths],
        [SMEM] + [VMEM] * SIDE,
        [VMEM] * (3 * SIDE),
        [],
        nbytes=8 << 20,
    )(pick, *home)
    own_part, next_part, far_part = summed[:SIDE], summed[SIDE : 2 * SIDE], summed[2 * SIDE :]
    far_part, next_part = lax.optimization_barrier((route(far_part), next_part))
    far_ends = join(far_part)
    next_part, own_part = lax.optimization_barrier((route(next_part), own_part))
    next_end = join(next_part, far_ends[0])[0]
    own_part = [
        own_part[0], shift(own_part[1], -1, 0), next_part[2][RB:], shift(own_part[3], -3, 0)
    ]
    ends = [swap_z(next_end, 1), swap_z(far_ends[0], 2), swap_z(far_ends[1], 3)]
    total = (ends[0][:RB] + ends[1][:RB]) + ends[2][:RB]
    total += (own_part[0] + own_part[1]) + (own_part[2] + own_part[3])
    tail = (far_ends[0][RB:] + ends[0][RB:]) + (ends[1][RB:] + ends[2][RB:])
    summed_back = total.transpose(1, 0, 2).reshape(width, nodes)
    h_grad = (root * summed_back + direct).T
    grad = tail.transpose(1, 0, 2).reshape(width, 4 * width)

    output = jnp.zeros((width, nodes), F32)
    for d in range(4):
        output = lax.dynamic_update_slice_in_dim(output, out[d], (own_col ^ d) * quarter, 1)
    return (output.T, h_grad, grad)


def solution(mesh):
    in_specs = (
        P("row", "col"),
        P(),
        P("row", "col"),
        P("row"),
        P("row", None, None),
        P("row"),
        P("row"),
        P("row"),
        P("row"),
        P(),
    )
    out_specs = (P("row", "col"), P("row", "col"), P("col", None))
    return jax.shard_map(
        on_device, mesh=mesh, in_specs=in_specs, out_specs=out_specs, check_vma=False
    )
```

```python
import functools

import jax
import jax.numpy as jnp
from jax import lax
from jax.experimental import pallas as pl
from jax.experimental.pallas import tpu as pltpu
from jax.sharding import PartitionSpec as P

SIDE = 4
RB = 8
GROUP = 32
CUTS = 4
PER = SIDE * SIDE * 2
F32 = jnp.float32
BF16 = jnp.bfloat16
NT = (((1,), (1,)), ((), ()))
NN = (((1,), (0,)), ((), ()))
TN = (((0,), (0,)), ((), ()))


def row_id(z, x, y):
    return z * SIDE * SIDE + x * SIDE + y


def shift(value, du, dv):
    pairs = []
    for row in range(SIDE**3):
        z, x, y = row // (SIDE * SIDE), row // SIDE % SIDE, row % SIDE
        for col in range(4):
            dx, dy = (dv, du) if col % 2 else (du, dv)
            pairs.append((row * 4 + col, row_id(z, (x + dx) % SIDE, (y + dy) % SIDE) * 4 + col))
    return lax.ppermute(value, ("row", "col"), pairs)


def swap_z(value, k):
    return lax.ppermute(value, "row", [(r, r ^ (k * SIDE * SIDE)) for r in range(SIDE**3)])


def swap_col(value, k):
    return lax.ppermute(value, "col", [(c, c ^ k) for c in range(4)])


def halves(value):
    high = value.astype(BF16)
    return high, (value - high.astype(F32)).astype(BF16)


def dot(a, b, dims):
    return lax.dot_general(a, b, dims, preferred_element_type=F32)


def dot3(a, b, dims):
    a_high, a_low = a
    b_high, b_low = b
    return dot(a_high, b_high, dims) + (dot(a_high, b_low, dims) + dot(a_low, b_high, dims))


def lanes(index, size):
    return pl.ds(pl.multiple_of(index * size, size), size)


def fetch(sources, targets, sems):
    copies = [
        pltpu.make_async_copy(source, target, sems.at[i])
        for i, (source, target) in enumerate(zip(sources, targets))
    ]
    for copy in copies:
        copy.start()
    return copies


def wait(copies):
    for copy in copies:
        copy.wait()


def convert_kernel(tiles, out, held, built, in_sems, out_sems):
    n = in_sems.shape[0]
    span = tiles.shape[0] // n
    cuts = [pl.ds(i * span, span) for i in range(n)]
    loads = fetch([tiles.at[c] for c in cuts], [held.at[c] for c in cuts], in_sems)
    copies = []
    for i, cut in enumerate(cuts):
        loads[i].wait()

        def one(t, carry):
            built[t] = held[t].astype(F32).astype(BF16)
            return carry

        lax.fori_loop(i * span, (i + 1) * span, one, 0, unroll=2)
        copy = pltpu.make_async_copy(built.at[cut], out.at[cut], out_sems.at[i])
        copy.start()
        copies.append(copy)
    wait(copies)


SPANS = ((0, RB), (RB, RB), (2 * RB, 2 * RB))


def pack_kernel(pick, *refs):
    n = SIDE * len(SPANS)
    ins, outs = refs[:n], refs[n : n + SIDE]
    for far in range(SIDE):
        for near in range(SIDE):
            for k in range(SIDE):
                source, base = ins[min(k, 2) * SIDE + near], RB * (k == 3)
                for p in range(2):
                    at = (near * SIDE + k) * 2 + p
                    outs[far][at] = source[base + pick[far * PER + at]]


def unpack_far_kernel(pick, *refs):
    ins, outs = refs[:SIDE], refs[SIDE:]
    for out in outs:
        out[...] = jnp.zeros_like(out)
    tail = (ins[0][PER:] + ins[1][PER:]) + (ins[2][PER:] + ins[3][PER:])
    for near in range(SIDE):
        outs[near][2 * RB :] = tail
        for k in (2, 3):
            for far in range(SIDE):
                for p in range(2):
                    at = (near * SIDE + k) * 2 + p
                    outs[near][RB * (k == 3) + pick[far * PER + at]] += ins[far][at]


def unpack_kernel(pick, *refs):
    ins, outs = refs[:SIDE], refs[SIDE:]
    for out in outs:
        out[...] = jnp.zeros_like(out)
    for near in range(SIDE):
        for k in range(2):
            target, base = outs[k * SIDE + near], 0
            if k == 0 and near == 2:
                target, base = outs[SIDE + near], RB
            for far in range(SIDE):
                for p in range(2):
                    at = (near * SIDE + k) * 2 + p
                    target[base + pick[far * PER + at]] += ins[far][at]


def join_kernel(count, *refs):
    n = SIDE if count == 2 else SIDE + 1
    ins, outs = refs[:n], refs[n:]
    for k, out in enumerate(outs):
        spans = [(pl.ds(0, RB), pl.ds(k * RB, RB))]
        if count == 2:
            spans.append((pl.ds(RB, 2), pl.ds(2 * RB, 2)))
        else:
            out[RB:] = ins[SIDE][RB:]
        for target, source in spans:
            out[target] = (ins[0][source] + ins[1][source]) + (ins[2][source] + ins[3][source])


def run_groups(group, count, span, tile_loads):
    groups = (count + GROUP - 1) // GROUP
    step = span // GROUP
    for i, load in enumerate(tile_loads):
        load.wait()
        lax.fori_loop(jnp.minimum(i * step, groups), jnp.minimum((i + 1) * step, groups), group, 0)


def forward_kernel(
    rows, at, info, scaled, root, tiles, q0, q1, q2, q3,
    o0, o1, o2, o3, held, blocks, total, tile_sems, sems,
):
    span = tiles.shape[0] // CUTS
    cuts = [pl.ds(i * span, span) for i in range(CUTS)]
    parts = (q0, q1, q2, q3)
    loads = fetch(parts, [blocks.at[pl.ds(i * PER, PER)] for i in range(SIDE)], sems)
    tile_loads = fetch([tiles.at[c] for c in cuts], [held.at[c] for c in cuts], tile_sems)
    total[...] = jnp.zeros_like(total)
    wait(loads)
    width = total.shape[1]

    def group(g, carry):
        first = g * GROUP
        sums = []
        for u in range(GROUP):
            pair = jnp.concatenate(halves(blocks[at[first + u]]), 0)
            both = dot(pair, held[first + u], NT)
            sums.append(both[:width] + both[width:])
        for u in range(GROUP):
            total[rows[first + u]] += sums[u]
        return carry

    run_groups(group, info[0], span, tile_loads)
    size = total.shape[2]
    own = info[1]
    for k, out in enumerate((o0, o1, o2, o3)):
        for h in range(2):
            b = (own ^ k) * 2 + h
            span = lanes(b, size)
            out[:, h * size : (h + 1) * size] = (total[b] + scaled[:, span]) * root[:, span]


def dense_kernel(
    scale, info, a0, a1, a2, a3, c0, c1, c2, c3, weight,
    b0, b1, b2, b3, y0, y1, y2, y3, work, work2,
):
    own = info[1]
    part = a0.shape[0]
    rows = [pl.ds(pl.multiple_of((own ^ k) * part, part), part) for k in range(4)]
    for k, (a, c) in enumerate(zip((a0, a1, a2, a3), (c0, c1, c2, c3))):
        work[rows[k], :] = a[...]
        work2[rows[k], :] = c[...]
    agg = halves(work[...])
    w = halves(weight[...])
    preact = dot3(w, agg, TN)
    gate = jax.nn.sigmoid(preact)
    delta = halves(work2[...] * gate * (1.0 + preact * (1.0 - gate)))
    work[...] = preact * gate
    for k, out in enumerate((y0, y1, y2, y3)):
        out[...] = work[rows[k], :]
    work2[...] = dot3(w, delta, NN)
    work[...] = dot3(agg, delta, NT) * scale
    for k, out in enumerate((b0, b1, b2, b3)):
        out[:part, :] = work2[rows[k], :]
        out[part:, :] = work[rows[k], :]


def backward_kernel(
    rows, at, info, root, inverse, i0, i1, i2, i3, tiles,
    direct, e0, e1, e2, e3, held, blocks, source, tail, tile_sems, sems, tail_sems,
):
    parts = (e0, e1, e2, e3)
    size = tiles.shape[2]
    width = i0.shape[0] // 2
    span = tiles.shape[0] // CUTS
    cuts = [pl.ds(i * span, span) for i in range(CUTS)]
    tile_loads = fetch([tiles.at[c] for c in cuts], [held.at[c] for c in cuts], tile_sems)
    for h in range(2):
        cols = slice(h * size, (h + 1) * size)
        tail[h] = (i0[width:, cols] + i1[width:, cols]) + (i2[width:, cols] + i3[width:, cols])
    tails = fetch([tail] * SIDE, [part.at[pl.ds(PER, 2)] for part in parts], tail_sems)
    blocks[...] = jnp.zeros_like(blocks)
    own = info[1]
    for k, piece in enumerate((i0, i1, i2, i3)):
        for h in range(2):
            b = (own ^ k) * 2 + h
            where = lanes(b, size)
            value = piece[:width, h * size : (h + 1) * size]
            direct[:, where] = value * inverse[:, where]
            source[b] = jnp.concatenate(halves(value * root[:, where]), 0)

    def group(g, carry):
        first = g * GROUP
        sums = []
        for u in range(GROUP):
            both = dot(source[rows[first + u]], held[first + u], NN)
            sums.append(both[:width] + both[width:])
        for u in range(GROUP):
            blocks[at[first + u]] += sums[u]
        return carry

    run_groups(group, info[0], span, tile_loads)
    sent = fetch(
        [blocks.at[pl.ds(i * PER, PER)] for i in range(SIDE)],
        [part.at[pl.ds(0, PER)] for part in parts],
        sems,
    )
    wait(sent)
    wait(tails)


VMEM = pl.BlockSpec(memory_space=pltpu.VMEM)
SMEM = pl.BlockSpec(memory_space=pltpu.SMEM)
HBM = pl.BlockSpec(memory_space=pltpu.HBM)
LIMIT = 40 * 1024 * 1024
DMA = pltpu.SemaphoreType.DMA


def struct(*shape):
    return jax.ShapeDtypeStruct(shape, F32)


def call(kernel, name, out_shape, in_specs, out_specs, scratch, nbytes=1 << 22):
    return pl.pallas_call(
        kernel,
        out_shape=out_shape,
        in_specs=in_specs,
        out_specs=out_specs,
        scratch_shapes=scratch,
        compiler_params=pltpu.CompilerParams(vmem_limit_bytes=LIMIT),
        cost_estimate=pl.CostEstimate(flops=0, bytes_accessed=nbytes, transcendentals=0),
        name=name,
    )


def on_device(
    features,
    weight,
    cotangent,
    degrees,
    tiles,
    block_rows,
    block_source,
    block_slot,
    block_count,
    pair_blocks,
):
    nodes, width = features.shape
    slots, size = tiles.shape[0], tiles.shape[1]
    quarter = nodes // 4
    n_row = lax.axis_size("row")
    own = lax.axis_index("row")
    own_col = lax.axis_index("col")
    turned = own_col % 2 == 1

    def place(row):
        x, y = row // SIDE % SIDE, row % SIDE
        return row // (SIDE * SIDE), jnp.where(turned, y, x), jnp.where(turned, x, y)

    def row_at(z, u, v):
        return jnp.where(turned, row_id(z, v % SIDE, u % SIDE), row_id(z, u % SIDE, v % SIDE))

    z, u, v = place(own)
    box = jnp.arange(SIDE, dtype=jnp.int32)

    degree_f = degrees.astype(F32)[None, :]
    root = lax.rsqrt(degree_f)
    inverse = 1.0 / degree_f
    features_t = features.T
    cotangent_t = cotangent.T

    far, near, deep = box[:, None, None], box[None, :, None], box[None, None, :]
    pick = pair_blocks[row_at(z, u, v + far), row_at(z ^ deep, u - near, v)].reshape(-1)

    live = jnp.arange(slots, dtype=jnp.int32) < block_count[0]
    from_z, from_u, from_v = place(block_source)
    at = (v - from_v) % SIDE * SIDE + (u - from_u) % SIDE
    at = (at * SIDE + (from_z ^ z)) * 2 + block_slot
    n_blocks = PER * SIDE
    rows_forward = jnp.where(live, block_rows, RB)
    at_back = jnp.where(live, at, n_blocks)
    info = jnp.stack([block_count[0], own_col.astype(jnp.int32)])

    def piece(value, d):
        return lax.dynamic_slice_in_dim(value, (own_col ^ d) * quarter, quarter, 1)

    def exchange(pieces):
        return [pieces[0]] + [swap_col(pieces[d], d) for d in (1, 2, 3)]

    shape = (PER, width, size)
    longer = (PER + 2, width, size)
    lengths = [
        size + 2 * (part == 2) + RB * (part == 1 and near == 2)
        for part, (_, size) in enumerate(SPANS)
        for near in range(SIDE)
    ]

    def spread(value):
        return [value] + [shift(value, d, 0) for d in (1, 2, 3)]

    def route(values):
        return [values[0]] + [shift(values[d], -d, 0) for d in (1, 2, 3)]

    def join(arrived, *more):
        count = 1 if more else 2
        return call(
            functools.partial(join_kernel, count),
            "join%d" % count,
            [struct(RB + 2, width, size)] * count,
            [VMEM] * (SIDE + len(more)),
            [VMEM] * count,
            [],
        )(*arrived, *more)

    scaled = features_t * root
    blocked = scaled.reshape(width, RB, size).transpose(1, 0, 2)
    deep = [blocked] + [swap_z(blocked, d) for d in range(1, SIDE)]
    adjacency = call(
        convert_kernel,
        "convert",
        jax.ShapeDtypeStruct(tiles.shape, BF16),
        [HBM],
        HBM,
        [pltpu.VMEM(tiles.shape, jnp.int32), pltpu.VMEM(tiles.shape, BF16), DMA((8,)), DMA((8,))],
        nbytes=12 << 20,
    )(tiles)
    cot = [piece(cotangent_t, d) for d in range(4)]
    later, pick = lax.optimization_barrier((blocked, pick))
    own_part = spread(later)
    next_part = spread(deep[1])
    own_part, next_part, far_deep, adjacency, pick, cot = lax.optimization_barrier(
        (own_part, next_part, deep[2:], adjacency, pick, cot)
    )
    far_part = spread(jnp.concatenate(far_deep))
    packed = call(
        pack_kernel,
        "pack",
        [struct(*shape)] * SIDE,
        [SMEM] + [VMEM] * (3 * SIDE),
        [VMEM] * SIDE,
        [],
        nbytes=8 << 20,
    )(pick, *own_part, *next_part, *far_part)
    cot, packed = lax.optimization_barrier((cot, packed))
    got = [packed[0]] + [shift(packed[d], 0, d) for d in (1, 2, 3)]
    cot = exchange(cot)
    got, cot = lax.optimization_barrier((got, cot))
    agg = call(
        forward_kernel,
        "forward",
        [struct(width, quarter)] * 4,
        [SMEM] * 3 + [VMEM] * 2 + [HBM] * (SIDE + 1),
        [VMEM] * 4,
        [
            pltpu.VMEM(tiles.shape, BF16),
            pltpu.VMEM((n_blocks, width, size), F32),
            pltpu.VMEM((RB + 1, width, size), F32),
            DMA((CUTS,)),
            DMA((SIDE,)),
        ],
        nbytes=16 << 20,
    )(rows_forward, at, info, scaled, root, adjacency, *got)
    agg = exchange(agg)
    dense = call(
        functools.partial(dense_kernel, (n_row * nodes) ** (-0.5)),
        "dense",
        [struct(2 * width, quarter)] * 4 + [struct(width, quarter)] * 4,
        [SMEM] + [VMEM] * 9,
        [VMEM] * 8,
        [pltpu.VMEM((4 * width, quarter), F32), pltpu.VMEM((4 * width, quarter), F32)],
    )(info, *agg, *cot, weight)
    back = exchange(dense[:4])

    direct, *sent = call(
        backward_kernel,
        "backward",
        [struct(width, nodes)] + [struct(*longer)] * SIDE,
        [SMEM] * 3 + [VMEM] * 6 + [HBM],
        [VMEM] + [HBM] * SIDE,
        [
            pltpu.VMEM(tiles.shape, BF16),
            pltpu.VMEM((n_blocks + 1, width, size), F32),
            pltpu.VMEM((RB, 2 * width, size), BF16),
            pltpu.VMEM((2, width, size), F32),
            DMA((CUTS,)),
            DMA((SIDE,)),
            DMA((SIDE,)),
        ],
        nbytes=16 << 20,
    )(block_rows, at_back, info, root, inverse, *back, adjacency)

    sent, out = lax.optimization_barrier((sent, dense[4:]))
    home = [sent[0]] + [shift(sent[d], 0, -d) for d in (1, 2, 3)]
    out = exchange(out)
    home, out = lax.optimization_barrier((home, out))
    far_part = call(
        unpack_far_kernel,
        "unpack_far",
        [struct(length, width, size) for length in lengths[2 * SIDE :]],
        [SMEM] + [VMEM] * SIDE,
        [VMEM] * SIDE,
        [],
    )(pick, *home)
    summed = call(
        unpack_kernel,
        "unpack",
        [struct(length, width, size) for length in lengths[: 2 * SIDE]],
        [SMEM] + [VMEM] * SIDE,
        [VMEM] * (2 * SIDE),
        [],
    )(pick, *home)
    own_part, next_part = summed[:SIDE], summed[SIDE:]
    far_part, next_part = lax.optimization_barrier((route(far_part), next_part))
    far_ends = join(far_part)
    next_part, own_part = lax.optimization_barrier((route(next_part), own_part))
    next_end = join(next_part, far_ends[0])[0]
    own_part = [
        own_part[0], shift(own_part[1], -1, 0), next_part[2][RB:], shift(own_part[3], -3, 0)
    ]
    ends = [swap_z(next_end, 1), swap_z(far_ends[0], 2), swap_z(far_ends[1], 3)]
    total = (ends[0][:RB] + ends[1][:RB]) + ends[2][:RB]
    total += (own_part[0] + own_part[1]) + (own_part[2] + own_part[3])
    tail = (far_ends[0][RB:] + ends[0][RB:]) + (ends[1][RB:] + ends[2][RB:])
    summed_back = total.transpose(1, 0, 2).reshape(width, nodes)
    h_grad = (root * summed_back + direct).T
    grad = tail.transpose(1, 0, 2).reshape(width, 4 * width)

    output = jnp.zeros((width, nodes), F32)
    for d in range(4):
        output = lax.dynamic_update_slice_in_dim(output, out[d], (own_col ^ d) * quarter, 1)
    return (output.T, h_grad, grad)


def solution(mesh):
    in_specs = (
        P("row", "col"),
        P(),
        P("row", "col"),
        P("row"),
        P("row", None, None),
        P("row"),
        P("row"),
        P("row"),
        P("row"),
        P(),
    )
    out_specs = (P("row", "col"), P("row", "col"), P("col", None))
    return jax.shard_map(
        on_device, mesh=mesh, in_specs=in_specs, out_specs=out_specs, check_vma=False
    )
```

```python
import functools

import jax
import jax.numpy as jnp
from jax import lax
from jax.experimental import pallas as pl
from jax.experimental.pallas import tpu as pltpu
from jax.sharding import PartitionSpec as P

SIDE = 4
RB = 8
GROUP = 64
CUTS = 2
PER = SIDE * SIDE * 2
F32 = jnp.float32
BF16 = jnp.bfloat16
NT = (((1,), (1,)), ((), ()))
NN = (((1,), (0,)), ((), ()))
TN = (((0,), (0,)), ((), ()))


def row_id(z, x, y):
    return z * SIDE * SIDE + x * SIDE + y


def shift(value, du, dv):
    pairs = []
    for row in range(SIDE**3):
        z, x, y = row // (SIDE * SIDE), row // SIDE % SIDE, row % SIDE
        for col in range(4):
            dx, dy = (dv, du) if col % 2 else (du, dv)
            pairs.append((row * 4 + col, row_id(z, (x + dx) % SIDE, (y + dy) % SIDE) * 4 + col))
    return lax.ppermute(value, ("row", "col"), pairs)


def swap_z(value, k):
    return lax.ppermute(value, "row", [(r, r ^ (k * SIDE * SIDE)) for r in range(SIDE**3)])


def swap_col(value, k):
    return lax.ppermute(value, "col", [(c, c ^ k) for c in range(4)])


def halves(value):
    high = value.astype(BF16)
    return high, (value - high.astype(F32)).astype(BF16)


def dot(a, b, dims):
    return lax.dot_general(a, b, dims, preferred_element_type=F32)


def dot3(a, b, dims):
    a_high, a_low = a
    b_high, b_low = b
    return dot(a_high, b_high, dims) + (dot(a_high, b_low, dims) + dot(a_low, b_high, dims))


def lanes(index, size):
    return pl.ds(pl.multiple_of(index * size, size), size)


def fetch(sources, targets, sems):
    copies = [
        pltpu.make_async_copy(source, target, sems.at[i])
        for i, (source, target) in enumerate(zip(sources, targets))
    ]
    for copy in copies:
        copy.start()
    return copies


def wait(copies):
    for copy in copies:
        copy.wait()


def convert_kernel(tiles, out, held, built, in_sems, out_sems):
    n = in_sems.shape[0]
    span = tiles.shape[0] // n
    cuts = [pl.ds(i * span, span) for i in range(n)]
    loads = fetch([tiles.at[c] for c in cuts], [held.at[c] for c in cuts], in_sems)
    copies = []
    for i, cut in enumerate(cuts):
        loads[i].wait()

        def one(t, carry):
            built[t] = held[t].astype(F32).astype(BF16)
            return carry

        lax.fori_loop(i * span, (i + 1) * span, one, 0, unroll=2)
        copy = pltpu.make_async_copy(built.at[cut], out.at[cut], out_sems.at[i])
        copy.start()
        copies.append(copy)
    wait(copies)


SPANS = ((0, RB), (RB, RB), (2 * RB, 2 * RB))


def pack_kernel(pick, *refs):
    n = SIDE * len(SPANS)
    ins, outs = refs[:n], refs[n : n + SIDE]
    for far in range(SIDE):
        for near in range(SIDE):
            for k in range(SIDE):
                source, base = ins[min(k, 2) * SIDE + near], RB * (k == 3)
                for p in range(2):
                    at = (near * SIDE + k) * 2 + p
                    outs[far][at] = source[base + pick[far * PER + at]]


def unpack_far_kernel(pick, *refs):
    ins, outs = refs[:SIDE], refs[SIDE:]
    for out in outs:
        out[...] = jnp.zeros_like(out)
    tail = (ins[0][PER:] + ins[1][PER:]) + (ins[2][PER:] + ins[3][PER:])
    for near in range(SIDE):
        outs[near][2 * RB :] = tail
        for k in (2, 3):
            for far in range(SIDE):
                for p in range(2):
                    at = (near * SIDE + k) * 2 + p
                    outs[near][RB * (k == 3) + pick[far * PER + at]] += ins[far][at]


def unpack_kernel(pick, *refs):
    ins, outs = refs[:SIDE], refs[SIDE:]
    for out in outs:
        out[...] = jnp.zeros_like(out)
    for near in range(SIDE):
        for k in range(2):
            target, base = outs[k * SIDE + near], 0
            if k == 0 and near == 2:
                target, base = outs[SIDE + near], RB
            for far in range(SIDE):
                for p in range(2):
                    at = (near * SIDE + k) * 2 + p
                    target[base + pick[far * PER + at]] += ins[far][at]


def join_kernel(count, *refs):
    n = SIDE if count == 2 else SIDE + 1
    ins, outs = refs[:n], refs[n:]
    for k, out in enumerate(outs):
        spans = [(pl.ds(0, RB), pl.ds(k * RB, RB))]
        if count == 2:
            spans.append((pl.ds(RB, 2), pl.ds(2 * RB, 2)))
        else:
            out[RB:] = ins[SIDE][RB:]
        for target, source in spans:
            out[target] = (ins[0][source] + ins[1][source]) + (ins[2][source] + ins[3][source])


def run_groups(group, count, span, tile_loads):
    groups = (count + GROUP - 1) // GROUP
    step = span // GROUP
    for i, load in enumerate(tile_loads):
        load.wait()
        lax.fori_loop(jnp.minimum(i * step, groups), jnp.minimum((i + 1) * step, groups), group, 0)


def forward_kernel(
    rows, at, info, scaled, root, tiles, q0, q1, q2, q3,
    o0, o1, o2, o3, held, blocks, total, tile_sems, sems,
):
    span = tiles.shape[0] // CUTS
    cuts = [pl.ds(i * span, span) for i in range(CUTS)]
    parts = (q0, q1, q2, q3)
    loads = fetch(parts, [blocks.at[pl.ds(i * PER, PER)] for i in range(SIDE)], sems)
    tile_loads = fetch([tiles.at[c] for c in cuts], [held.at[c] for c in cuts], tile_sems)
    total[...] = jnp.zeros_like(total)
    wait(loads)
    width = total.shape[1]

    def group(g, carry):
        first = g * GROUP
        sums = []
        for u in range(GROUP):
            pair = jnp.concatenate(halves(blocks[at[first + u]]), 0)
            both = dot(pair, held[first + u], NT)
            sums.append(both[:width] + both[width:])
        for u in range(GROUP):
            total[rows[first + u]] += sums[u]
        return carry

    run_groups(group, info[0], span, tile_loads)
    size = total.shape[2]
    own = info[1]
    for k, out in enumerate((o0, o1, o2, o3)):
        for h in range(2):
            b = (own ^ k) * 2 + h
            span = lanes(b, size)
            out[:, h * size : (h + 1) * size] = (total[b] + scaled[:, span]) * root[:, span]


def dense_kernel(
    scale, info, a0, a1, a2, a3, c0, c1, c2, c3, weight,
    b0, b1, b2, b3, y0, y1, y2, y3, work, work2,
):
    own = info[1]
    part = a0.shape[0]
    rows = [pl.ds(pl.multiple_of((own ^ k) * part, part), part) for k in range(4)]
    for k, (a, c) in enumerate(zip((a0, a1, a2, a3), (c0, c1, c2, c3))):
        work[rows[k], :] = a[...]
        work2[rows[k], :] = c[...]
    agg = halves(work[...])
    w = halves(weight[...])
    preact = dot3(w, agg, TN)
    gate = jax.nn.sigmoid(preact)
    delta = halves(work2[...] * gate * (1.0 + preact * (1.0 - gate)))
    work[...] = preact * gate
    for k, out in enumerate((y0, y1, y2, y3)):
        out[...] = work[rows[k], :]
    work2[...] = dot3(w, delta, NN)
    work[...] = dot3(agg, delta, NT) * scale
    for k, out in enumerate((b0, b1, b2, b3)):
        out[:part, :] = work2[rows[k], :]
        out[part:, :] = work[rows[k], :]


def backward_kernel(
    rows, at, info, root, inverse, i0, i1, i2, i3, tiles,
    direct, e0, e1, e2, e3, held, blocks, source, tail, tile_sems, sems, tail_sems,
):
    parts = (e0, e1, e2, e3)
    size = tiles.shape[2]
    width = i0.shape[0] // 2
    span = tiles.shape[0] // CUTS
    cuts = [pl.ds(i * span, span) for i in range(CUTS)]
    tile_loads = fetch([tiles.at[c] for c in cuts], [held.at[c] for c in cuts], tile_sems)
    for h in range(2):
        cols = slice(h * size, (h + 1) * size)
        tail[h] = (i0[width:, cols] + i1[width:, cols]) + (i2[width:, cols] + i3[width:, cols])
    tails = fetch([tail] * SIDE, [part.at[pl.ds(PER, 2)] for part in parts], tail_sems)
    blocks[...] = jnp.zeros_like(blocks)
    own = info[1]
    for k, piece in enumerate((i0, i1, i2, i3)):
        for h in range(2):
            b = (own ^ k) * 2 + h
            where = lanes(b, size)
            value = piece[:width, h * size : (h + 1) * size]
            direct[:, where] = value * inverse[:, where]
            source[b] = jnp.concatenate(halves(value * root[:, where]), 0)

    def group(g, carry):
        first = g * GROUP
        sums = []
        for u in range(GROUP):
            both = dot(source[rows[first + u]], held[first + u], NN)
            sums.append(both[:width] + both[width:])
        for u in range(GROUP):
            blocks[at[first + u]] += sums[u]
        return carry

    run_groups(group, info[0], span, tile_loads)
    sent = fetch(
        [blocks.at[pl.ds(i * PER, PER)] for i in range(SIDE)],
        [part.at[pl.ds(0, PER)] for part in parts],
        sems,
    )
    wait(sent)
    wait(tails)


VMEM = pl.BlockSpec(memory_space=pltpu.VMEM)
SMEM = pl.BlockSpec(memory_space=pltpu.SMEM)
HBM = pl.BlockSpec(memory_space=pltpu.HBM)
LIMIT = 40 * 1024 * 1024
DMA = pltpu.SemaphoreType.DMA


def struct(*shape):
    return jax.ShapeDtypeStruct(shape, F32)


def call(kernel, name, out_shape, in_specs, out_specs, scratch, nbytes=1 << 22):
    return pl.pallas_call(
        kernel,
        out_shape=out_shape,
        in_specs=in_specs,
        out_specs=out_specs,
        scratch_shapes=scratch,
        compiler_params=pltpu.CompilerParams(vmem_limit_bytes=LIMIT),
        cost_estimate=pl.CostEstimate(flops=0, bytes_accessed=nbytes, transcendentals=0),
        name=name,
    )


def on_device(
    features,
    weight,
    cotangent,
    degrees,
    tiles,
    block_rows,
    block_source,
    block_slot,
    block_count,
    pair_blocks,
):
    nodes, width = features.shape
    slots, size = tiles.shape[0], tiles.shape[1]
    quarter = nodes // 4
    n_row = lax.axis_size("row")
    own = lax.axis_index("row")
    own_col = lax.axis_index("col")
    turned = own_col % 2 == 1

    def place(row):
        x, y = row // SIDE % SIDE, row % SIDE
        return row // (SIDE * SIDE), jnp.where(turned, y, x), jnp.where(turned, x, y)

    def row_at(z, u, v):
        return jnp.where(turned, row_id(z, v % SIDE, u % SIDE), row_id(z, u % SIDE, v % SIDE))

    z, u, v = place(own)
    box = jnp.arange(SIDE, dtype=jnp.int32)

    degree_f = degrees.astype(F32)[None, :]
    root = lax.rsqrt(degree_f)
    inverse = 1.0 / degree_f
    features_t = features.T
    cotangent_t = cotangent.T

    far, near, deep = box[:, None, None], box[None, :, None], box[None, None, :]
    pick = pair_blocks[row_at(z, u, v + far), row_at(z ^ deep, u - near, v)].reshape(-1)

    live = jnp.arange(slots, dtype=jnp.int32) < block_count[0]
    from_z, from_u, from_v = place(block_source)
    at = (v - from_v) % SIDE * SIDE + (u - from_u) % SIDE
    at = (at * SIDE + (from_z ^ z)) * 2 + block_slot
    n_blocks = PER * SIDE
    rows_forward = jnp.where(live, block_rows, RB)
    at_back = jnp.where(live, at, n_blocks)
    info = jnp.stack([block_count[0], own_col.astype(jnp.int32)])

    def piece(value, d):
        return lax.dynamic_slice_in_dim(value, (own_col ^ d) * quarter, quarter, 1)

    def exchange(pieces):
        return [pieces[0]] + [swap_col(pieces[d], d) for d in (1, 2, 3)]

    shape = (PER, width, size)
    longer = (PER + 2, width, size)
    lengths = [
        size + 2 * (part == 2) + RB * (part == 1 and near == 2)
        for part, (_, size) in enumerate(SPANS)
        for near in range(SIDE)
    ]

    def spread(value):
        return [value] + [shift(value, d, 0) for d in (1, 2, 3)]

    def route(values):
        return [values[0]] + [shift(values[d], -d, 0) for d in (1, 2, 3)]

    def join(arrived, *more):
        count = 1 if more else 2
        return call(
            functools.partial(join_kernel, count),
            "join%d" % count,
            [struct(RB + 2, width, size)] * count,
            [VMEM] * (SIDE + len(more)),
            [VMEM] * count,
            [],
        )(*arrived, *more)

    scaled = features_t * root
    blocked = scaled.reshape(width, RB, size).transpose(1, 0, 2)
    deep = [blocked] + [swap_z(blocked, d) for d in range(1, SIDE)]
    adjacency = call(
        convert_kernel,
        "convert",
        jax.ShapeDtypeStruct(tiles.shape, BF16),
        [HBM],
        HBM,
        [pltpu.VMEM(tiles.shape, jnp.int32), pltpu.VMEM(tiles.shape, BF16), DMA((8,)), DMA((8,))],
        nbytes=12 << 20,
    )(tiles)
    cot = [piece(cotangent_t, d) for d in range(4)]
    later, pick = lax.optimization_barrier((blocked, pick))
    own_part = spread(later)
    next_part = spread(deep[1])
    own_part, next_part, far_deep, adjacency, pick, cot = lax.optimization_barrier(
        (own_part, next_part, deep[2:], adjacency, pick, cot)
    )
    far_part = spread(jnp.concatenate(far_deep))
    packed = call(
        pack_kernel,
        "pack",
        [struct(*shape)] * SIDE,
        [SMEM] + [VMEM] * (3 * SIDE),
        [VMEM] * SIDE,
        [],
        nbytes=8 << 20,
    )(pick, *own_part, *next_part, *far_part)
    cot, packed = lax.optimization_barrier((cot, packed))
    got = [packed[0]] + [shift(packed[d], 0, d) for d in (1, 2, 3)]
    cot = exchange(cot)
    got, cot = lax.optimization_barrier((got, cot))
    agg = call(
        forward_kernel,
        "forward",
        [struct(width, quarter)] * 4,
        [SMEM] * 3 + [VMEM] * 2 + [HBM] * (SIDE + 1),
        [VMEM] * 4,
        [
            pltpu.VMEM(tiles.shape, BF16),
            pltpu.VMEM((n_blocks, width, size), F32),
            pltpu.VMEM((RB + 1, width, size), F32),
            DMA((CUTS,)),
            DMA((SIDE,)),
        ],
        nbytes=16 << 20,
    )(rows_forward, at, info, scaled, root, adjacency, *got)
    agg = exchange(agg)
    dense = call(
        functools.partial(dense_kernel, (n_row * nodes) ** (-0.5)),
        "dense",
        [struct(2 * width, quarter)] * 4 + [struct(width, quarter)] * 4,
        [SMEM] + [VMEM] * 9,
        [VMEM] * 8,
        [pltpu.VMEM((4 * width, quarter), F32), pltpu.VMEM((4 * width, quarter), F32)],
    )(info, *agg, *cot, weight)
    back = exchange(dense[:4])

    direct, *sent = call(
        backward_kernel,
        "backward",
        [struct(width, nodes)] + [struct(*longer)] * SIDE,
        [SMEM] * 3 + [VMEM] * 6 + [HBM],
        [VMEM] + [HBM] * SIDE,
        [
            pltpu.VMEM(tiles.shape, BF16),
            pltpu.VMEM((n_blocks + 1, width, size), F32),
            pltpu.VMEM((RB, 2 * width, size), BF16),
            pltpu.VMEM((2, width, size), F32),
            DMA((CUTS,)),
            DMA((SIDE,)),
            DMA((SIDE,)),
        ],
        nbytes=16 << 20,
    )(block_rows, at_back, info, root, inverse, *back, adjacency)

    sent, out = lax.optimization_barrier((sent, dense[4:]))
    home = [sent[0]] + [shift(sent[d], 0, -d) for d in (1, 2, 3)]
    out = exchange(out)
    home, out = lax.optimization_barrier((home, out))
    far_part = call(
        unpack_far_kernel,
        "unpack_far",
        [struct(length, width, size) for length in lengths[2 * SIDE :]],
        [SMEM] + [VMEM] * SIDE,
        [VMEM] * SIDE,
        [],
    )(pick, *home)
    summed = call(
        unpack_kernel,
        "unpack",
        [struct(length, width, size) for length in lengths[: 2 * SIDE]],
        [SMEM] + [VMEM] * SIDE,
        [VMEM] * (2 * SIDE),
        [],
    )(pick, *home)
    own_part, next_part = summed[:SIDE], summed[SIDE:]
    far_part, next_part = lax.optimization_barrier((route(far_part), next_part))
    far_ends = join(far_part)
    next_part, own_part = lax.optimization_barrier((route(next_part), own_part))
    next_end = join(next_part, far_ends[0])[0]
    own_part = [
        own_part[0], shift(own_part[1], -1, 0), next_part[2][RB:], shift(own_part[3], -3, 0)
    ]
    ends = [swap_z(next_end, 1), swap_z(far_ends[0], 2), swap_z(far_ends[1], 3)]
    total = (ends[0][:RB] + ends[1][:RB]) + ends[2][:RB]
    total += (own_part[0] + own_part[1]) + (own_part[2] + own_part[3])
    tail = (far_ends[0][RB:] + ends[0][RB:]) + (ends[1][RB:] + ends[2][RB:])
    summed_back = total.transpose(1, 0, 2).reshape(width, nodes)
    h_grad = (root * summed_back + direct).T
    grad = tail.transpose(1, 0, 2).reshape(width, 4 * width)

    output = jnp.zeros((width, nodes), F32)
    for d in range(4):
        output = lax.dynamic_update_slice_in_dim(output, out[d], (own_col ^ d) * quarter, 1)
    return (output.T, h_grad, grad)


def solution(mesh):
    in_specs = (
        P("row", "col"),
        P(),
        P("row", "col"),
        P("row"),
        P("row", None, None),
        P("row"),
        P("row"),
        P("row"),
        P("row"),
        P(),
    )
    out_specs = (P("row", "col"), P("row", "col"), P("col", None))
    return jax.shard_map(
        on_device, mesh=mesh, in_specs=in_specs, out_specs=out_specs, check_vma=False
    )
```
